512 devices in a mesh: queue: 64 (over z_lo, y, core), space: 8 (over x, z_hi).
Axes of the slice: x: 4, y: 8, z: 8 (z_hi: 2, z_lo: 4; z = z_hi * 4 + z_lo), core: 2. Of those that a mesh axis runs over, the one named last changes fastest.
Arguments:
- latents: float32 [64, 384, 16], P('queue', 'space'), may hold values from -6 to 6
- fresh_noise: float32 [2, 384, 16], P(None, 'space'), may hold values from -6 to 6
- levels: int32 [64], replicated, may hold values from 1 to 1000, as said below
- modulation_weight: bfloat16 [256, 6912], P(None, 'space'), may hold values from -0.375 to 0.375
- embed_weight: bfloat16 [16, 1152], replicated, may hold values from -1.5 to 1.5
- attention_weights: bfloat16 [8, 1152, 1152], P(None, 'space')
- final_weight: bfloat16 [1152, 16], replicated, may hold values from -0.1875 to 0.1875
Outputs:
- queue_after: float32 [64, 384, 16], P('queue', 'space')
- velocity: float32 [2, 64, 384, 16], P(None, 'queue', 'space')
The draws below stay inside these ranges and needn't reach their ends.
Inputs may be any that keep to these rules, and one draw needn't show every extreme that they name: levels rise strictly along the queue, and the last one is 1000.
All inputs are finite; a program needn't handle non-finite values.
Results may differ from the reference program's by a relative error of at most 0.034.
Values may be sent and summed in bfloat16 or wider, within the bound.
A program may use at most 64 MiB of HBM per device.

```python
import math
import jax
import jax.numpy as jnp
from jax import lax

D = 1152
HEAD = 72
HEADS = 16
CH = 16
FREQ = 256
STEPS = 2
REACH = 4
LEVELS = 1000
INNER = 1152
NB = 64
S_ALL = 384
HGROUPS = 8


def draw_levels(key, part):
    key = jax.random.fold_in(key, 7)
    increments = jax.random.randint(key, (NB - 1,), 1, LEVELS // NB + 1)
    rising = jnp.cumsum(increments)
    return jnp.concatenate([rising, jnp.full((1,), LEVELS, jnp.int32)]).astype(jnp.int32)


def draw_attention_weights(key, part):
    key = jax.random.fold_in(key, 11)
    base = jax.random.normal(key, (8, INNER, D), jnp.float32)
    input_scale = D ** (-0.5)
    output_scale = INNER ** (-0.5)
    matrices = [base[index] * (output_scale if index % 4 == 3 else input_scale) for index in range(8)]
    return jnp.stack(matrices, 0).astype(jnp.bfloat16)


def block_scale(own_key, shape, shards, smallest, largest):
    gain, own = 1.0, jax.random.fold_in(own_key, 6)
    for axis_at, shards_of in shards:
        heights = jnp.exp(jax.random.uniform(jax.random.fold_in(own, axis_at), (shards_of,), jnp.float32, smallest / len(shards), largest / len(shards)))
        gain = gain * jnp.repeat(heights, shape[axis_at] // shards_of).reshape([-1 if axis == axis_at else 1 for axis in range(len(shape))])
    return gain


def scatter_about(key, dims, deviation, bound, pieces=(), held_as=jnp.bfloat16):
    gain = block_scale(key, dims, pieces, -0.22, 0.18) if pieces else 1.0
    drawn = jax.random.normal(key, dims, jnp.float32) * deviation * gain
    return jnp.minimum(jnp.maximum(drawn, -bound), bound).astype(held_as)


def setup_inputs(seed: int = 0) -> dict:
    seeds = jax.random.split(jax.random.key(seed), 8)
    return {
        "latents": scatter_about(seeds[0], (NB, S_ALL, CH), 1.0, 6.0, ((0, 64), (1, 8)), jnp.float32),
        "fresh_noise": scatter_about(seeds[1], (STEPS, S_ALL, CH), 1.0, 6.0, ((1, 8),), jnp.float32),
        "levels": draw_levels(jax.random.fold_in(seeds[7], 71), 0),
        "modulation_weight": scatter_about(seeds[3], (FREQ, 6 * D), FREQ ** -0.5, 0.375, ((1, 8),)),
        "embed_weight": scatter_about(seeds[4], (CH, D), CH ** -0.5, 1.5),
        "attention_weights": draw_attention_weights(jax.random.fold_in(seeds[7], 71), 0),
        "final_weight": scatter_about(seeds[6], (D, CH), D ** -0.5, 0.1875),
    }


def layer_norm(values):
    average = lax.optimization_barrier(jnp.mean(values, -1, keepdims=True))
    centred = values - average
    variance = lax.optimization_barrier(jnp.mean(centred * centred, -1, keepdims=True))
    return centred * lax.rsqrt(variance + 1e-06)

def time_features(level_values):
    times = level_values.astype(jnp.float32) / LEVELS
    half_size = FREQ // 2
    frequency = jnp.exp(-math.log(10000.0) * jnp.arange(half_size).astype(jnp.float32) / half_size)
    angles = (times * 1000.0)[:, None] * frequency[None, :]
    return jnp.concatenate([jnp.cos(angles), jnp.sin(angles)], -1).astype(jnp.bfloat16)

def spatial_attend(query, key_rows, values):
    scores = jnp.einsum('qhd,khd->hqk', query.astype(jnp.float32), key_rows.astype(jnp.float32)) * (1.0 / math.sqrt(HEAD))
    probabilities = jax.nn.softmax(scores, axis=-1).astype(jnp.bfloat16)
    return jnp.einsum('hqk,khd->qhd', probabilities.astype(jnp.float32), values.astype(jnp.float32)).astype(jnp.bfloat16)

def temporal_attend(query, key_rows, values, usable):
    scores = jnp.einsum('shd,gshd->shg', query.astype(jnp.float32), key_rows.astype(jnp.float32)) * (1.0 / math.sqrt(HEAD))
    scores = jnp.where(usable[None, None, :], scores, -1e+30)
    probabilities = jax.nn.softmax(scores, axis=-1).astype(jnp.bfloat16)
    return jnp.einsum('shg,gshd->shd', probabilities.astype(jnp.float32), values.astype(jnp.float32)).astype(jnp.bfloat16)

def grouped_output(attended, exit_weight):
    group_width = INNER // HGROUPS
    total = jnp.zeros((attended.shape[0], exit_weight.shape[1]), jnp.float32)
    for group in range(HGROUPS):
        first = group * group_width
        product = jnp.dot(attended[:, first:first + group_width], exit_weight[first:first + group_width, :], preferred_element_type=jnp.float32)
        total = total + lax.optimization_barrier(product.astype(jnp.bfloat16)).astype(jnp.float32)
    return total

def denoise(current, conditioning, attention_weights, embed_weight, final_weight):
    block_count, token_count, channels = current.shape
    width = embed_weight.shape[1]
    conditioning = conditioning[:, None, :]

    def project(index, source):
        result = jnp.dot(source.reshape(-1, width), attention_weights[index].T, preferred_element_type=jnp.float32)
        return result.astype(jnp.bfloat16).reshape(block_count, token_count, HEADS, HEAD)
    stream_in = jnp.dot(current.astype(jnp.bfloat16).reshape(-1, channels), embed_weight, preferred_element_type=jnp.float32)
    stream_in = stream_in.reshape(block_count, token_count, width)
    normed = (layer_norm(stream_in) * (1.0 + conditioning[..., width:2 * width]) + conditioning[..., 0:width]).astype(jnp.bfloat16)
    spatial = lax.map(lambda group: spatial_attend(group[0], group[1], group[2]), (project(0, normed), project(1, normed), project(2, normed)))
    spatial_sum = grouped_output(spatial.reshape(-1, INNER), attention_weights[3]).reshape(block_count, token_count, width)
    stream_mid = stream_in + conditioning[..., 2 * width:3 * width] * spatial_sum
    normed_temporal = (layer_norm(stream_mid) * (1.0 + conditioning[..., 4 * width:5 * width]) + conditioning[..., 3 * width:4 * width]).astype(jnp.bfloat16)
    temporal_query = project(4, normed_temporal)
    key_padded = jnp.pad(project(5, normed_temporal), ((REACH, REACH), (0, 0), (0, 0), (0, 0)))
    value_padded = jnp.pad(project(6, normed_temporal), ((REACH, REACH), (0, 0), (0, 0), (0, 0)))

    def one_block(index):
        key_rows = lax.dynamic_slice_in_dim(key_padded, index, 2 * REACH + 1, 0)
        values = lax.dynamic_slice_in_dim(value_padded, index, 2 * REACH + 1, 0)
        offsets = jnp.arange(2 * REACH + 1).astype(jnp.int32) - REACH + index
        usable = (offsets >= 0) & (offsets < block_count)
        query = lax.dynamic_index_in_dim(temporal_query, index, 0, keepdims=False)
        return temporal_attend(query, key_rows, values, usable)
    temporal = lax.map(one_block, jnp.arange(block_count).astype(jnp.int32))
    temporal_sum = grouped_output(temporal.reshape(-1, INNER), attention_weights[7]).reshape(block_count, token_count, width)
    stream_out = stream_mid + conditioning[..., 5 * width:6 * width] * temporal_sum
    velocity = jnp.dot(layer_norm(stream_out).astype(jnp.bfloat16).reshape(-1, width), final_weight, preferred_element_type=jnp.float32)
    return velocity.reshape(block_count, token_count, channels)

def reference(latents, fresh_noise, levels, modulation_weight, embed_weight, attention_weights, final_weight):
    conditioning = jnp.dot(time_features(levels), modulation_weight, preferred_element_type=jnp.float32)
    lower = jnp.concatenate([jnp.zeros((1,), jnp.int32), levels[:-1].astype(jnp.int32)])
    step_size = (lower - levels.astype(jnp.int32)).astype(jnp.float32) / LEVELS
    current = latents
    velocities = []
    for iteration in range(STEPS):
        velocity = denoise(current, conditioning, attention_weights, embed_weight, final_weight)
        velocities.append(velocity)
        updated = current + step_size[:, None, None] * velocity
        current = jnp.concatenate([updated[1:], fresh_noise[iteration][None]], 0)
    return (current, jnp.stack(velocities, 0))
```

```python
import functools
import math

import jax
import jax.numpy as jnp
from jax import lax
from jax.experimental import pallas as pl
from jax.experimental.pallas import tpu as pltpu
from jax.sharding import PartitionSpec as P

HEAD = 72
FREQ = 256
STEPS = 2
REACH = 4
LEVELS = 1000
D = 1152
ROWS = 48
NX = 4
NY = 8
SPACE = 8
ROUNDS = 4
THIRD = 384
WINDOW = 2 * REACH + 1
SCALE = 1.0 / math.sqrt(HEAD)
MESH = pl.DeviceIdType.MESH
F32 = jnp.float32
BF16 = jnp.bfloat16
PEERS = [(dx, dz) for dx in range(NX) for dz in range(2) if (dx, dz) != (0, 0)]
PARTS = [(1, 3), (6, 2), (4, 2)]
CHIPS = [-2, -1, 1, 2]


def time_features(level_values):
    times = level_values.astype(F32) / LEVELS
    half_size = FREQ // 2
    frequency = jnp.exp(-math.log(10000.0) * jnp.arange(half_size).astype(F32) / half_size)
    angles = (times * 1000.0)[:, None] * frequency[None, :]
    return jnp.concatenate([jnp.cos(angles), jnp.sin(angles)], -1).astype(BF16)


def layer_norm(values):
    average = jnp.mean(values, -1, keepdims=True)
    centred = values - average
    variance = jnp.mean(centred * centred, -1, keepdims=True)
    return centred * lax.rsqrt(variance + 1e-06)


def dot(a, b):
    return lax.dot_general(a, b, (((1,), (0,)), ((), ())), preferred_element_type=F32)


def dot_t(a, b):
    return lax.dot_general(a, b, (((1,), (1,)), ((), ())), preferred_element_type=F32)


def kernel(
    nq,
    lat, fresh, feat, step_size, mw, emb, fin, aw,
    after, velocity,
    wf, ws, tok, zf, zcur, mods, mstage, mline, mvec, n1s, qs, ks, vs, a1s, a1r,
    h1s, n2b, q2s, a2s, hm, hmt, ub, us,
    lsem, lat_s, lat_r, mod_s, mod_r, z_s, z_r, x_s, x_r, f_s, f_r, y_s, y_r, c_s, c_r,
    a_s, a_r, n_s, n_r, b_s, b_r, u_s, u_r, v_s, v_r,
):
    q = lax.axis_index("queue")
    s = lax.axis_index("space")
    x, zh = lax.div(s, 2), lax.rem(s, 2)
    chip, core = lax.div(q, 2), lax.rem(q, 2)
    line, y = lax.div(chip, NY), lax.rem(chip, NY)
    parity = lax.rem(y, 2)
    chips = nq // 2

    def peer(dx, dz):
        return lax.rem(x + dx, NX) * 2 + lax.rem(zh + dz, 2)

    def along_y(by):
        return (line * NY + lax.rem(y + by + NY, NY)) * 2 + core

    sibling = chip * 2 + 1 - core
    ahead, behind = along_y(1 - 2 * core), along_y(2 * core - 1)
    sends = []

    def remote(src, dst, ss, rs, to_q, to_s):
        return pltpu.make_async_remote_copy(
            src_ref=src, dst_ref=dst, send_sem=ss, recv_sem=rs,
            device_id=(to_q, to_s), device_id_type=MESH,
        )

    def send(src, dst, ss, rs, to_q, to_s, when=None):
        copy = remote(src, dst, ss, rs, to_q, to_s)
        if when is None:
            copy.start()
        else:
            pl.when(when)(copy.start)
        sends.append((copy, when))

    def arrived(dst, rs, when=None):
        copy = remote(dst, dst, rs, rs, q, s)
        if when is None:
            copy.wait_recv()
        else:
            pl.when(when)(copy.wait_recv)

    loads = [pltpu.make_async_copy(aw.at[pl.ds(0, 3)], ws, lsem.at[5])]
    for m in range(5):
        loads.append(
            pltpu.make_async_copy(aw.at[3 + m], wf.at[pl.ds(3 * m, 3), 0], lsem.at[m])
        )
    for load in loads[1:]:
        load.start()
    loads[0].start()

    barrier = pltpu.get_barrier_semaphore()

    def signal(to_q, to_s):
        pl.semaphore_signal(barrier, inc=1, device_id=(to_q, to_s), device_id_type=MESH)

    for dx, dz in PEERS:
        signal(q, peer(dx, dz))
    signal(behind, s)
    signal(sibling, s)
    expected = len(PEERS) + 2
    for dc in CHIPS:
        there = (chip + dc >= 0) & (chip + dc < chips)

        @pl.when(there)
        def _(dc=dc):
            signal((chip + dc) * 2 + core, s)

        expected = expected + there.astype(jnp.int32)

    @pl.when(q < nq - 1)
    def _():
        for dx in range(NX):
            for dz in range(2):
                signal(q + 1, peer(dx, dz))

    expected = expected + jnp.where(q > 0, SPACE, 0)

    tok[0, 0] = lat[...].astype(BF16)
    zcur[...] = lat[...]
    wf[15, 0] = jnp.zeros((ROWS, D), BF16)
    mstage[...] = jnp.zeros_like(mstage)
    mstage[:, 0:864] = dot(feat[...], mw[...])
    shift = lax.rem(s * 864, D)
    mline[...] = pltpu.roll(mstage[...], shift, 1)[0:1, :]
    for t in range(3):
        for ref, (row, lane) in ((hm, (0, 1)), (hmt, (1, 0))):
            shape = ref.shape[1:]
            place = lax.broadcasted_iota(jnp.int32, shape, row)
            head = lax.broadcasted_iota(jnp.int32, shape, lane)
            at = place - (head >> 1) * ROWS
            second = (at + t * ROWS >= HEAD).astype(jnp.int32)
            ref[t] = jnp.where((at >= 0) & (at < ROWS) & (second == (head & 1)), 1.0, 0.0).astype(BF16)
    for dc in CHIPS:
        @pl.when((chip + dc < 0) | (chip + dc >= chips))
        def _(dc=dc):
            for step in range(STEPS):
                for c in range(2):
                    n2b[step, (dc + 2) * 2 + c] = jnp.zeros((ROWS, D), BF16)

    pl.semaphore_wait(barrier, expected)

    for i, (dx, dz) in enumerate(PEERS):
        back = ((-dx) % NX) * 2 + dz
        send(tok.at[0, 0], tok.at[0, back], lat_s.at[i], lat_r.at[back], q, peer(dx, dz))
    for i, (dx, dz) in enumerate(PEERS):
        back = ((-dx) % NX) * 2 + dz
        send(mline, mods.at[s], mod_s.at[i], mod_r.at[back], q, peer(dx, dz))
    mods[s] = mline[...]

    def chunk(i, p, c):
        return 4 * i + 2 * p + c

    def first(i):
        j = chunk(i, parity, core)
        send(wf.at[j, 0], wf.at[j, 1], z_s.at[i], z_r.at[i], q, peer(0, 1))
        send(wf.at[j, 0], wf.at[j, 6], x_s.at[i, 0, 0], x_r.at[i, 0, 0], q, peer(1, 0))
        send(wf.at[j, 0], wf.at[j, 2], x_s.at[i, 0, 1], x_r.at[i, 0, 1], q, peer(3, 0))

    def second(i):
        j = chunk(i, parity, core)
        arrived(wf.at[j, 1], z_r.at[i])
        send(wf.at[j, 1], wf.at[j, 7], x_s.at[i, 1, 0], x_r.at[i, 1, 0], q, peer(1, 0))
        send(wf.at[j, 1], wf.at[j, 3], x_s.at[i, 1, 1], x_r.at[i, 1, 1], q, peer(3, 0))

    def third(i):
        j = chunk(i, parity, core)
        start = 6 - 4 * core
        arrived(wf.at[j, start], x_r.at[i, 0, core])
        arrived(wf.at[j, start + 1], x_r.at[i, 1, core])
        to = lax.rem(x + 1 + 2 * core, NX) * 2 + zh
        send(wf.at[j, pl.ds(start, 2)], wf.at[j, pl.ds(4, 2)], f_s.at[i], f_r.at[i], q, to)

    def share(i, part):
        j = chunk(i, parity, core)
        at = pl.ds(*PARTS[part])
        send(wf.at[j, at], wf.at[j, at], y_s.at[i, part], y_r.at[i, part], ahead, s)
        send(wf.at[j, at], wf.at[j, at], c_s.at[i, part], c_r.at[i, part], sibling, s)

    def fourth(i):
        j = chunk(i, parity, core)
        start = 2 + 4 * core
        arrived(wf.at[j, start], x_r.at[i, 0, 1 - core])
        arrived(wf.at[j, start + 1], x_r.at[i, 1, 1 - core])
        share(i, 0)
        share(i, 1)

    def fifth(i):
        j = chunk(i, parity, core)
        arrived(wf.at[j, pl.ds(4, 2)], f_r.at[i])
        share(i, 2)

    def sixth(i):
        j = chunk(i, 1 - parity, core)
        for part in range(3):
            at = pl.ds(*PARTS[part])
            arrived(wf.at[j, at], y_r.at[i, part])
            send(wf.at[j, at], wf.at[j, at], c_s.at[i, 3 + part], c_r.at[i, 3 + part], sibling, s)

    def seventh(i):
        for half, p in ((0, parity), (3, 1 - parity)):
            j = chunk(i, p, 1 - core)
            for part in range(3):
                arrived(wf.at[j, pl.ds(*PARTS[part])], c_r.at[i, half + part])

    for load in loads[1:]:
        load.wait()
    first(0)
    first(1)

    for dx, dz in PEERS:
        arrived(mods.at[peer(dx, dz)], mod_r.at[dx * 2 + dz])
    for base in (0, 4):
        piece = base // 4 * 3
        left = [mods[base + g][:, 0:D] for g in range(4)]
        right = [mods[base + g][:, D : 2 * D] for g in range(4)]
        mvec[piece] = left[0] + left[1]
        mvec[piece + 1] = right[1] + left[2]
        mvec[piece + 2] = right[2] + left[3]

    loads[0].wait()
    for dx, dz in PEERS:
        arrived(tok.at[0, dx * 2 + dz], lat_r.at[dx * 2 + dz])

    lane = lax.broadcasted_iota(jnp.int32, (1, 144), 1)
    in_first = lane < HEAD

    def spatial(step):
        @pl.loop(0, SPACE)
        def _(r):
            h0 = dot(tok[step, r], emb[...])
            n1 = layer_norm(h0) * (1.0 + mvec[1]) + mvec[0]
            n1s[r] = n1.astype(BF16)

        for index, ref in enumerate((qs, ks, vs)):
            ref[...] = dot_t(
                n1s[...].reshape(SPACE * ROWS, D), ws[index].reshape(144, D)
            ).astype(BF16)

    def attend(step):
        @pl.loop(0, 4)
        def _(b):
            rows = pl.ds(pl.multiple_of(b * 96, 96), 96)
            query = qs[rows, :]
            heads = []
            for h in range(2):
                mine = in_first if h == 0 else ~in_first
                scores = dot_t(jnp.where(mine, query, jnp.zeros_like(query)), ks[...]) * SCALE
                e = jnp.exp(scores - jnp.max(scores, -1, keepdims=True))
                p = (e / jnp.sum(e, -1, keepdims=True)).astype(BF16)
                heads.append(dot(p, vs[...]))
            a1 = jnp.where(in_first, heads[0], heads[1]).astype(BF16)
            a1s[step, pl.ds(b * 2, 2)] = a1.reshape(2, ROWS, 144)

        for i, (dx, dz) in enumerate(PEERS):
            back = ((-dx) % NX) * 2 + dz
            send(a1s.at[step, dx * 2 + dz], a1r.at[step, back],
                 a_s.at[step, i], a_r.at[step, back], q, peer(dx, dz))
        a1r[step, 0] = a1s[step, 0]

    def leave(step):
        for dx, dz in PEERS:
            arrived(a1r.at[step, dx * 2 + dz], a_r.at[step, dx * 2 + dz])

    def middle(step):
        o1 = dot(a1r[step, 0], wf[0:3, 0].reshape(144, D))
        for r in range(1, SPACE):
            o1 = o1 + dot(a1r[step, r], wf[0:3, r].reshape(144, D))
        h1 = dot(tok[step, 0], emb[...]) + mvec[2] * o1
        h1s[...] = h1
        n2 = layer_norm(h1) * (1.0 + mvec[4]) + mvec[3]
        n2b[step, 4 + core] = n2.astype(BF16)
        for i, dc in enumerate(CHIPS):
            there = (chip + dc >= 0) & (chip + dc < chips)
            own = n2b.at[step, 4 + core]
            send(own, n2b.at[step, (2 - dc) * 2 + core], n_s.at[step, i], n_r.at[step, 3 - i],
                 (chip + dc) * 2 + core, s, there)
        send(n2b.at[step, 4 + core], n2b.at[step, 4 + core], b_s.at[step, 4], b_r.at[step, 4], sibling, s)

    def around(step):
        order = [1, 2, 0, 3]
        for i in order:
            dc = CHIPS[i]
            there = (chip + dc >= 0) & (chip + dc < chips)
            slot = (dc + 2) * 2 + core
            arrived(n2b.at[step, slot], n_r.at[step, i], there)
            wanted = there
            if dc == -2:
                wanted = there & (core == 1)
            if dc == 2:
                wanted = there & (core == 0)
            send(n2b.at[step, slot], n2b.at[step, slot], b_s.at[step, i], b_r.at[step, i],
                 sibling, s, wanted)
        arrived(n2b.at[step, 5 - core], b_r.at[step, 4])
        for i in order:
            dc = CHIPS[i]
            there = (chip + dc >= 0) & (chip + dc < chips)
            slot = (dc + 2) * 2 + 1 - core
            wanted = there
            if dc == -2:
                wanted = there & (core == 0)
            if dc == 2:
                wanted = there & (core == 1)
            arrived(n2b.at[step, slot], b_r.at[step, i], wanted)

    def queries(step):
        @pl.loop(0, 3)
        def _(t):
            q2s[t] = dot_t(n2b[step, 4 + core], wf[3 + t].reshape(THIRD, D)).astype(BF16)

    def temporal(step):
        window = n2b[step, pl.ds(core, WINDOW)].reshape(WINDOW * ROWS, D)

        def keys(t, total):
            k2 = dot_t(window, wf[6 + t].reshape(THIRD, D)).astype(BF16)
            product = k2.reshape(WINDOW, ROWS, THIRD).astype(F32) * q2s[t].astype(F32)[None]
            return total + dot(product.astype(BF16).reshape(WINDOW * ROWS, THIRD), hm[t])

        scores = lax.fori_loop(0, 3, keys, jnp.zeros((WINDOW * ROWS, 128), F32)) * SCALE
        scores = scores.reshape(WINDOW, ROWS, 128)
        block = lax.broadcasted_iota(jnp.int32, scores.shape, 0) - REACH + q
        scores = jnp.where((block >= 0) & (block < nq), scores, -1e30)
        e = jnp.exp(scores - jnp.max(scores, 0, keepdims=True))
        p = (e / jnp.sum(e, 0, keepdims=True)).astype(BF16).reshape(WINDOW * ROWS, 128)

        @pl.loop(0, 3)
        def _(t):
            v2 = dot_t(window, wf[9 + t].reshape(THIRD, D)).astype(BF16).astype(F32)
            spread = dot(p, hmt[t])
            a2s[t] = jnp.sum((spread * v2).reshape(WINDOW, ROWS, THIRD), 0).astype(BF16)

    def final(step):
        o2 = dot(a2s[0], wf[12].reshape(THIRD, D))
        for t in range(1, 3):
            o2 = o2 + dot(a2s[t], wf[12 + t].reshape(THIRD, D))
        h2 = h1s[...] + mvec[5] * o2
        v = dot(layer_norm(h2).astype(BF16), fin[...])
        velocity[step] = v
        u = zcur[...] + step_size[0:1, 0:1] * v
        us[step] = u
        head = q > 0
        tail = q == nq - 1
        if step < STEPS - 1:
            ub[0] = u.astype(BF16)
            ub[1] = fresh[step].astype(BF16)
            for dx in range(NX):
                for dz in range(2):
                    back = ((-dx) % NX) * 2 + dz
                    here = dx * 2 + dz
                    send(ub.at[0], tok.at[step + 1, back], u_s.at[0, here], u_r.at[back],
                         q - 1, peer(dx, dz), head)
                    if here:
                        send(ub.at[1], tok.at[step + 1, back], u_s.at[1, here], u_r.at[back],
                             q, peer(dx, dz), tail)
        send(us.at[step], zf.at[step], v_s.at[step], v_r.at[step], q - 1, s, head)

    def arrive(step):
        tail = q == nq - 1
        if step < STEPS - 1:
            for here in range(1, SPACE):
                arrived(tok.at[step + 1, here], u_r.at[here])
            arrived(tok.at[step + 1, 0], u_r.at[0], ~tail)

            @pl.when(tail)
            def _():
                tok[step + 1, 0] = fresh[step].astype(BF16)

        arrived(zf.at[step], v_r.at[step], ~tail)

        @pl.when(tail)
        def _():
            zf[step] = fresh[step]

    spatial(0)
    second(0)
    third(0)
    first(2)
    attend(0)
    fourth(0)
    second(1)
    fifth(0)
    third(1)
    first(3)
    leave(0)
    sixth(0)
    fourth(1)
    second(2)
    fifth(1)
    third(2)
    seventh(0)
    middle(0)
    sixth(1)
    fourth(2)
    second(3)
    fifth(2)
    third(3)
    seventh(1)
    queries(0)
    around(0)
    fourth(3)
    sixth(2)
    fifth(3)
    seventh(2)
    temporal(0)
    sixth(3)
    seventh(3)
    final(0)
    arrive(0)
    zcur[...] = zf[0]
    spatial(1)
    attend(1)
    leave(1)
    middle(1)
    queries(1)
    around(1)
    temporal(1)
    final(1)
    arrive(1)
    after[...] = zf[1]

    for copy, when in sends:
        if when is None:
            copy.wait_send()
        else:
            pl.when(when)(copy.wait_send)


def solution(mesh):
    nq = mesh.shape["queue"]

    def local(latents, fresh_noise, levels, modulation_weight, embed_weight, attention_weights, final_weight):
        q = lax.axis_index("queue")
        own = lax.dynamic_index_in_dim(levels, q, keepdims=False)
        below = lax.dynamic_index_in_dim(levels, jnp.maximum(q - 1, 0), keepdims=False)
        below = jnp.where(q > 0, below, 0)
        step_size = jnp.broadcast_to((below - own).astype(F32) / LEVELS, (8, 128))
        feat = jnp.broadcast_to(time_features(own.reshape(1)), (8, FREQ))
        dma = pltpu.SemaphoreType.DMA
        vmem = pl.BlockSpec(memory_space=pltpu.VMEM)
        after, velocity = pl.pallas_call(
            functools.partial(kernel, nq),
            out_shape=(
                jax.ShapeDtypeStruct((ROWS, 16), F32),
                jax.ShapeDtypeStruct((STEPS, ROWS, 16), F32),
            ),
            in_specs=[vmem] * 7 + [pl.BlockSpec(memory_space=pl.ANY)],
            out_specs=(vmem, vmem),
            scratch_shapes=[
                pltpu.VMEM((16, SPACE, ROWS, D), BF16),
                pltpu.VMEM((3, 3, ROWS, D), BF16),
                pltpu.VMEM((STEPS, SPACE, ROWS, 16), BF16),
                pltpu.VMEM((STEPS, ROWS, 16), F32),
                pltpu.VMEM((ROWS, 16), F32),
                pltpu.VMEM((SPACE, 1, 2 * D), F32),
                pltpu.VMEM((8, 2 * D), F32),
                pltpu.VMEM((1, 2 * D), F32),
                pltpu.VMEM((6, 1, D), F32),
                pltpu.VMEM((SPACE, ROWS, D), BF16),
                pltpu.VMEM((SPACE * ROWS, 144), BF16),
                pltpu.VMEM((SPACE * ROWS, 144), BF16),
                pltpu.VMEM((SPACE * ROWS, 144), BF16),
                pltpu.VMEM((STEPS, SPACE, ROWS, 144), BF16),
                pltpu.VMEM((STEPS, SPACE, ROWS, 144), BF16),
                pltpu.VMEM((ROWS, D), F32),
                pltpu.VMEM((STEPS, 10, ROWS, D), BF16),
                pltpu.VMEM((3, ROWS, THIRD), BF16),
                pltpu.VMEM((3, ROWS, THIRD), BF16),
                pltpu.VMEM((3, THIRD, 128), BF16),
                pltpu.VMEM((3, 128, THIRD), BF16),
                pltpu.VMEM((2, ROWS, 16), BF16),
                pltpu.VMEM((STEPS, ROWS, 16), F32),
                dma((6,)),
                dma((7,)), dma((SPACE,)),
                dma((7,)), dma((SPACE,)),
                dma((ROUNDS,)), dma((ROUNDS,)),
                dma((ROUNDS, 2, 2)), dma((ROUNDS, 2, 2)),
                dma((ROUNDS,)), dma((ROUNDS,)),
                dma((ROUNDS, 3)), dma((ROUNDS, 3)),
                dma((ROUNDS, 6)), dma((ROUNDS, 6)),
                dma((STEPS, 7)), dma((STEPS, SPACE)),
                dma((STEPS, 4)), dma((STEPS, 4)),
                dma((STEPS, 5)), dma((STEPS, 5)),
                dma((2, SPACE)), dma((SPACE,)),
                dma((STEPS,)), dma((STEPS,)),
            ],
            compiler_params=pltpu.CompilerParams(
                collective_id=0, has_side_effects=True, vmem_limit_bytes=56 << 20
            ),
            name="denoise",
        )(
            latents[0], fresh_noise, feat, step_size, modulation_weight, embed_weight,
            final_weight, attention_weights.reshape(8, 3, ROWS, D),
        )
        return after[None], velocity[:, None]

    in_specs = (
        P("queue", "space", None),
        P(None, "space", None),
        P(),
        P(None, "space"),
        P(),
        P(None, "space", None),
        P(),
    )
    out_specs = (P("queue", "space", None), P(None, "queue", "space", None))
    return jax.shard_map(local, mesh=mesh, in_specs=in_specs, out_specs=out_specs, check_vma=False)
```

```python
import functools
import math

import jax
import jax.numpy as jnp
from jax import lax
from jax.experimental import pallas as pl
from jax.experimental.pallas import tpu as pltpu
from jax.sharding import PartitionSpec as P

HEAD = 72
FREQ = 256
STEPS = 2
REACH = 4
LEVELS = 1000
D = 1152
ROWS = 48
NX = 4
NY = 8
SPACE = 8
ROUNDS = 4
THIRD = 384
SLOTS = 2 * REACH + 2
SCALE = 1.0 / math.sqrt(HEAD)
MESH = pl.DeviceIdType.MESH
F32 = jnp.float32
BF16 = jnp.bfloat16
SLOT = {(dx, dz): dz * NX + at for dz in range(2) for at, dx in enumerate((0, 3, 1, 2))}
PEERS = [place for place in SLOT if place != (0, 0)]
PARTS = [(1, 2), (3, 1), (4, 1), (5, 2), (7, 1)]
OVER_Z = (2, 4)
CHIPS = [-2, -1, 1, 2]


def time_features(level):
    half_size = FREQ // 2
    places = lax.broadcasted_iota(jnp.int32, (8, half_size), 1).astype(F32)
    frequency = jnp.exp(-math.log(10000.0) * places / half_size)
    angles = (level.astype(F32) / LEVELS * 1000.0) * frequency
    return jnp.concatenate([jnp.cos(angles), jnp.sin(angles)], -1).astype(BF16)


def layer_norm(values):
    average = jnp.mean(values, -1, keepdims=True)
    centred = values - average
    variance = jnp.mean(centred * centred, -1, keepdims=True)
    return centred * lax.rsqrt(variance + 1e-06)


def dot(a, b):
    return lax.dot_general(a, b, (((1,), (0,)), ((), ())), preferred_element_type=F32)


def t_dot(a, b):
    return lax.dot_general(a, b, (((0,), (0,)), ((), ())), preferred_element_type=F32)


def dot_t(a, b):
    return lax.dot_general(a, b, (((1,), (1,)), ((), ())), preferred_element_type=F32)


def kernel(
    nq,
    levels, lat, fresh, mw, emb, fin, aw,
    after, velocity,
    wf, ws, tok, zf, zcur, mods, mstage, mline, mvec, n1s, qs, ks, vs, a1s, a1r,
    h1s, n2b, q2s, a2s, sc, v2s, hm, hmt, ub, us,
    lsem, lat_s, lat_r, mod_s, mod_r, z_s, z_r, x_s, x_r, f_s, f_r, y_s, y_r, c_s, c_r,
    a_s, a_r, n_s, n_r, b_s, b_r, u_s, u_r, v_s, v_r,
):
    q = lax.axis_index("queue")
    s = lax.axis_index("space")
    x, zh = lax.div(s, 2), lax.rem(s, 2)
    chip, core = lax.div(q, 2), lax.rem(q, 2)
    line, y = lax.div(chip, NY), lax.rem(chip, NY)
    parity = lax.rem(y + line, 2)
    chips = nq // 2

    def peer(dx, dz):
        return lax.rem(x + dx, NX) * 2 + lax.rem(zh + dz, 2)

    def along_y(by):
        return (line * NY + lax.rem(y + by + NY, NY)) * 2 + core

    sibling = chip * 2 + 1 - core
    lines = nq // (2 * NY)
    mirror = ((lines - 1 - line) * NY + y) * 2 + core
    beside = ((line + 1 - 2 * lax.rem(line, 2)) * NY + y) * 2 + core
    ahead, behind = along_y(1 - 2 * core), along_y(2 * core - 1)
    sends = []

    def remote(src, dst, ss, rs, to_q, to_s):
        return pltpu.make_async_remote_copy(
            src_ref=src, dst_ref=dst, send_sem=ss, recv_sem=rs,
            device_id=(to_q, to_s), device_id_type=MESH,
        )

    def send(src, dst, ss, rs, to_q, to_s, when=None):
        copy = remote(src, dst, ss, rs, to_q, to_s)
        if when is None:
            copy.start()
        else:
            pl.when(when)(copy.start)
        sends.append((copy, when))

    def arrived(dst, rs, when=None):
        copy = remote(dst, dst, rs, rs, q, s)
        if when is None:
            copy.wait_recv()
        else:
            pl.when(when)(copy.wait_recv)

    loads = [pltpu.make_async_copy(aw.at[pl.ds(0, 3)], ws, lsem.at[5])]
    for m in range(5):
        loads.append(
            pltpu.make_async_copy(aw.at[3 + m], wf.at[pl.ds(3 * m, 3), 0], lsem.at[m])
        )
    for load in loads[1:]:
        load.start()
    loads[0].start()

    barrier = pltpu.get_barrier_semaphore()

    def signal(to_q, to_s):
        pl.semaphore_signal(barrier, inc=1, device_id=(to_q, to_s), device_id_type=MESH)

    for dx, dz in PEERS:
        signal(q, peer(dx, dz))
    signal(behind, s)
    signal(beside, s)
    signal(sibling, s)
    signal(mirror, peer(0, 1))
    expected = len(PEERS) + 4
    for dc in CHIPS:
        there = (chip + dc >= 0) & (chip + dc < chips)

        @pl.when(there)
        def _(dc=dc):
            signal((chip + dc) * 2 + core, s)

        expected = expected + there.astype(jnp.int32)

    @pl.when(q < nq - 1)
    def _():
        for dx in range(NX):
            for dz in range(2):
                signal(q + 1, peer(dx, dz))

    expected = expected + jnp.where(q > 0, SPACE, 0)

    tok[0, 0] = lat[...].astype(BF16)
    zcur[...] = lat[...]
    wf[15, 0] = jnp.zeros((ROWS, D), BF16)
    mstage[...] = jnp.zeros_like(mstage)
    mstage[:, 0:864] = dot_t(time_features(levels[q]), mw[...])
    shift = lax.rem(s * 864, D)
    mline[...] = pltpu.roll(mstage[...], shift, 1)[0:1, :]
    for t in range(3):
        for ref, (row, lane) in ((hm, (0, 1)), (hmt, (1, 0))):
            shape = ref.shape[1:]
            place = lax.broadcasted_iota(jnp.int32, shape, row)
            head = lax.broadcasted_iota(jnp.int32, shape, lane)
            at = place - (head >> 1) * ROWS
            second = (at + t * ROWS >= HEAD).astype(jnp.int32)
            ref[t] = jnp.where((at >= 0) & (at < ROWS) & (second == (head & 1)), 1.0, 0.0).astype(BF16)
    for step in range(STEPS):
        n2b[step, 9 - 9 * core] = jnp.zeros((ROWS, D), BF16)
    for dc in CHIPS:
        @pl.when((chip + dc < 0) | (chip + dc >= chips))
        def _(dc=dc):
            for step in range(STEPS):
                for c in range(2):
                    n2b[step, (dc + 2) * 2 + c] = jnp.zeros((ROWS, D), BF16)

    pl.semaphore_wait(barrier, expected)

    for i, (dx, dz) in enumerate(PEERS):
        back = SLOT[-dx % NX, dz]
        send(tok.at[0, 0], tok.at[0, back], lat_s.at[i], lat_r.at[back], q, peer(dx, dz))
    for i, (dx, dz) in enumerate(PEERS):
        back = SLOT[-dx % NX, dz]
        send(mline, mods.at[s], mod_s.at[i], mod_r.at[back], q, peer(dx, dz))
    mods[s] = mline[...]

    def chunk(i, p, c):
        return 4 * i + 2 * p + c

    def own_out(i):
        j = chunk(i, parity, core)
        send(wf.at[j, 0], wf.at[j, 1], x_s.at[i, 0, 0], x_r.at[i, 0, 0], q, peer(1, 0))
        send(wf.at[j, 0], wf.at[j, 2], x_s.at[i, 0, 1], x_r.at[i, 0, 1], q, peer(3, 0))

    def cross_out(i):
        j = chunk(i, 1 - parity, core)
        send(wf.at[j, 0], wf.at[j, 4], z_s.at[i], z_r.at[i], mirror, peer(0, 1))

    def share(i, part):
        j = chunk(i, parity, core)
        at = pl.ds(*PARTS[part])
        to = beside if part in OVER_Z else ahead
        send(wf.at[j, at], wf.at[j, at], y_s.at[i, part], y_r.at[i, part], to, s)
        send(wf.at[j, at], wf.at[j, at], c_s.at[i, part], c_r.at[i, part], sibling, s)

    def onward(i, half):
        j = chunk(i, parity, core)
        base = 4 * half
        arrived(wf.at[j, base + 1], x_r.at[i, half, 0])
        arrived(wf.at[j, base + 2], x_r.at[i, half, 1])
        to = lax.rem(x + 1 + 2 * core, NX) * 2 + zh
        send(wf.at[j, base + 1 + core], wf.at[j, base + 3], f_s.at[i, half], f_r.at[i, half], q, to)
        share(i, 3 * half)

    def far_in(i, half):
        j = chunk(i, parity, core)
        arrived(wf.at[j, 4 * half + 3], f_r.at[i, half])
        share(i, 3 * half + 1)

    def cross_in(i):
        j = chunk(i, parity, core)
        arrived(wf.at[j, 4], z_r.at[i])
        send(wf.at[j, 4], wf.at[j, 5], x_s.at[i, 1, 0], x_r.at[i, 1, 0], q, peer(1, 0))
        send(wf.at[j, 4], wf.at[j, 6], x_s.at[i, 1, 1], x_r.at[i, 1, 1], q, peer(3, 0))
        share(i, 2)

    def pass_on(i, *parts):
        j = chunk(i, 1 - parity, core)
        for part in parts:
            at = pl.ds(*PARTS[part])
            arrived(wf.at[j, at], y_r.at[i, part])
            send(wf.at[j, at], wf.at[j, at], c_s.at[i, 5 + part], c_r.at[i, 5 + part], sibling, s)

    def complete(i):
        for half, p in ((0, parity), (5, 1 - parity)):
            j = chunk(i, p, 1 - core)
            for part in range(5):
                arrived(wf.at[j, pl.ds(*PARTS[part])], c_r.at[i, half + part])

    for load in loads[1:]:
        load.wait()
    own_out(0)
    cross_out(0)
    own_out(1)
    own_out(2)
    own_out(3)

    for dx, dz in PEERS:
        arrived(mods.at[peer(dx, dz)], mod_r.at[SLOT[dx, dz]])
    for base in (0, 4):
        piece = base // 4 * 3
        left = [mods[base + g][:, 0:D] for g in range(4)]
        right = [mods[base + g][:, D : 2 * D] for g in range(4)]
        mvec[piece] = left[0] + left[1]
        mvec[piece + 1] = right[1] + left[2]
        mvec[piece + 2] = right[2] + left[3]

    loads[0].wait()
    lane = lax.broadcasted_iota(jnp.int32, (1, 144), 1)
    in_first = lane < HEAD

    def embed(step, *slots):
        for r in slots:
            if step == 0 and r:
                arrived(tok.at[0, r], lat_r.at[r])
            elif r:
                arrived(tok.at[step, r], u_r.at[r])
            elif step:
                arrived(tok.at[step, 0], u_r.at[0], q < nq - 1)

                @pl.when(q == nq - 1)
                def _():
                    tok[step, 0] = fresh[step - 1].astype(BF16)

            h0 = t_dot(tok[step, r], emb[...])
            n1s[r] = (layer_norm(h0) * (1.0 + mvec[1]) + mvec[0]).astype(BF16)

    def project(*indices):
        for index in indices:
            (qs, ks, vs)[index][...] = dot_t(
                n1s[...].reshape(SPACE * ROWS, D), ws[index].reshape(144, D)
            ).astype(BF16)

    def attend(step, b):
        query = qs[b * 96 : b * 96 + 96, :]
        heads = []
        for h in range(2):
            mine = in_first if h == 0 else ~in_first
            scores = dot_t(jnp.where(mine, query, jnp.zeros_like(query)), ks[...]) * SCALE
            e = jnp.exp(scores - jnp.max(scores, -1, keepdims=True))
            p = (e * (1.0 / jnp.sum(e, -1, keepdims=True))).astype(BF16)
            heads.append(dot(p, vs[...]))
        a1 = jnp.where(in_first, heads[0], heads[1]).astype(BF16)
        a1s[step, 2 * b : 2 * b + 2] = a1.reshape(2, ROWS, 144)
        for i, (dx, dz) in enumerate(PEERS):
            if SLOT[dx, dz] // 2 == b:
                back = SLOT[-dx % NX, dz]
                send(a1s.at[step, SLOT[dx, dz]], a1r.at[step, back],
                     a_s.at[step, i], a_r.at[step, back], q, peer(dx, dz))
        if b == 0:
            a1r[step, 0] = a1s[step, 0]

    def middle(step):
        h0 = t_dot(tok[step, 0], emb[...])
        o1 = dot(a1r[step, 0], wf[0:3, 0].reshape(144, D))
        for r in range(1, SPACE):
            arrived(a1r.at[step, r], a_r.at[step, r])
            o1 = o1 + dot(a1r[step, r], wf[0:3, r].reshape(144, D))
        h1 = h0 + mvec[2] * o1
        h1s[...] = h1
        n2 = layer_norm(h1) * (1.0 + mvec[4]) + mvec[3]
        n2b[step, 4 + core] = n2.astype(BF16)
        own = n2b.at[step, 4 + core]
        send(own, own, b_s.at[step, 4], b_r.at[step, 4], sibling, s)
        for i in (1, 2, 0, 3):
            dc = CHIPS[i]
            there = (chip + dc >= 0) & (chip + dc < chips)
            send(own, n2b.at[step, (2 - dc) * 2 + core], n_s.at[step, i], n_r.at[step, 3 - i],
                 (chip + dc) * 2 + core, s, there)

    def relay(step, *chips_from):
        for i in chips_from:
            dc = CHIPS[i]
            there = (chip + dc >= 0) & (chip + dc < chips)
            slot = (dc + 2) * 2 + core
            arrived(n2b.at[step, slot], n_r.at[step, i], there)
            wanted = there
            if dc == -2:
                wanted = there & (core == 1)
            if dc == 2:
                wanted = there & (core == 0)
            send(n2b.at[step, slot], n2b.at[step, slot], b_s.at[step, i], b_r.at[step, i],
                 sibling, s, wanted)

    def relayed(step, *chips_from):
        for i in chips_from:
            dc = CHIPS[i]
            there = (chip + dc >= 0) & (chip + dc < chips)
            slot = (dc + 2) * 2 + 1 - core
            wanted = there
            if dc == -2:
                wanted = there & (core == 0)
            if dc == 2:
                wanted = there & (core == 1)
            arrived(n2b.at[step, slot], b_r.at[step, i], wanted)

    def queries(step):
        for t in range(3):
            q2s[t] = dot_t(n2b[step, 4 + core], wf[3 + t].reshape(THIRD, D)).astype(BF16)
        arrived(n2b.at[step, 5 - core], b_r.at[step, 4])

    def keys(step, *groups):
        for low, high in groups:
            count = high - low
            rows = n2b[step, low:high].reshape(count * ROWS, D)
            total = jnp.zeros((count * ROWS, 128), F32)
            for t in range(3):
                k2 = dot_t(rows, wf[6 + t].reshape(THIRD, D)).astype(BF16)
                product = k2.reshape(count, ROWS, THIRD).astype(F32) * q2s[t].astype(F32)[None]
                total = total + dot(product.astype(BF16).reshape(count * ROWS, THIRD), hm[t])
            sc[low:high] = total.reshape(count, ROWS, 128)

    def values(step, *groups):
        for low, high in groups:
            count = high - low
            rows = n2b[step, low:high].reshape(count * ROWS, D)
            for t in range(3):
                v2 = dot_t(rows, wf[9 + t].reshape(THIRD, D)).astype(BF16)
                v2s[t, low:high] = v2.reshape(count, ROWS, THIRD)

    def blend():
        scores = sc[...] * SCALE
        block = lax.broadcasted_iota(jnp.int32, scores.shape, 0) + 2 * chip - REACH
        usable = (block >= 0) & (block < nq) & (block >= q - REACH) & (block <= q + REACH)
        scores = jnp.where(usable, scores, -1e30)
        e = jnp.exp(scores - jnp.max(scores, 0, keepdims=True))
        p = (e * (1.0 / jnp.sum(e, 0, keepdims=True))).astype(BF16).reshape(SLOTS * ROWS, 128)
        for t in range(3):
            spread = dot(p, hmt[t]).reshape(SLOTS, ROWS, THIRD)
            a2s[t] = jnp.sum(spread * v2s[t].astype(F32), 0).astype(BF16)

    def final(step):
        o2 = dot(a2s[0], wf[12].reshape(THIRD, D))
        for t in range(1, 3):
            o2 = o2 + dot(a2s[t], wf[12 + t].reshape(THIRD, D))
        h2 = h1s[...] + mvec[5] * o2
        v = dot_t(fin[...], layer_norm(h2).astype(BF16))
        velocity[step] = v
        below = jnp.where(q > 0, levels[jnp.maximum(q - 1, 0)], 0)
        u = zcur[...] + ((below - levels[q]).astype(F32) / LEVELS) * v
        us[step] = u
        head = q > 0
        tail = q == nq - 1
        if step < STEPS - 1:
            ub[0] = u.astype(BF16)
            ub[1] = fresh[step].astype(BF16)
            for dx in range(NX):
                for dz in range(2):
                    back = SLOT[-dx % NX, dz]
                    here = SLOT[dx, dz]
                    send(ub.at[0], tok.at[step + 1, back], u_s.at[0, here], u_r.at[back],
                         q - 1, peer(dx, dz), head)
                    if here:
                        send(ub.at[1], tok.at[step + 1, back], u_s.at[1, here], u_r.at[back],
                             q, peer(dx, dz), tail)
        send(us.at[step], zf.at[step], v_s.at[step], v_r.at[step], q - 1, s, head)

    def arrive(step):
        arrived(zf.at[step], v_r.at[step], q < nq - 1)

        @pl.when(q == nq - 1)
        def _():
            zf[step] = fresh[step]

    cross_out(1)
    embed(0,0,1,2,3)
    onward(0,0)
    onward(1,0)
    embed(0,4,5,6,7)
    cross_in(0)
    cross_out(2)
    project(0)
    pass_on(0,0)
    far_in(0,0)
    project(1,2)
    pass_on(1,0)
    far_in(1,0)
    attend(0,2)
    onward(2,0)
    cross_in(1)
    cross_out(3)
    attend(0,3)
    onward(0,1)
    pass_on(0,1,2)
    attend(0,1)
    pass_on(1,1)
    far_in(2,0)
    pass_on(2,0)
    attend(0,0)
    far_in(0,1)
    pass_on(1,2)
    onward(3,0)
    cross_in(2)
    onward(1,1)
    pass_on(0,3)
    far_in(1,1)
    pass_on(0,4)
    pass_on(2,1,2)
    cross_in(3)
    pass_on(3,0)
    far_in(3,0)
    onward(2,1)
    pass_on(1,3)
    complete(0)
    middle(0)
    pass_on(3,1)
    pass_on(1,4)
    far_in(2,1)
    onward(3,1)
    pass_on(3,2)
    pass_on(2,3)
    complete(1)
    queries(0)
    relay(0,1,2)
    far_in(3,1)
    pass_on(2,4)
    complete(2)
    relay(0,0,3)
    relayed(0,1,2,0,3)
    keys(0,(0,10))
    pass_on(3,3)
    values(0,(0,10))
    pass_on(3,4)
    blend()
    complete(3)
    final(0)
    embed(1, 0, 1, 2, 3, 4, 5, 6, 7)
    project(0, 1, 2)
    attend(1, 2)
    attend(1, 3)
    attend(1, 1)
    attend(1, 0)
    arrive(0)
    zcur[...] = zf[0]
    middle(1)
    queries(1)
    keys(1, (4, 6))
    values(1, (4, 6))
    relay(1, 1, 2)
    relayed(1, 1, 2)
    keys(1, (2, 4), (6, 8))
    relay(1, 0, 3)
    values(1, (2, 4), (6, 8))
    relayed(1, 0, 3)
    keys(1, (0, 2), (8, 10))
    values(1, (0, 2), (8, 10))
    blend()
    final(1)
    arrive(1)
    after[...] = zf[1]

    for copy, when in sends:
        if when is None:
            copy.wait_send()
        else:
            pl.when(when)(copy.wait_send)


def solution(mesh):
    nq = mesh.shape["queue"]

    def local(latents, fresh_noise, levels, modulation_weight, embed_weight, attention_weights, final_weight):
        dma = pltpu.SemaphoreType.DMA
        vmem = pl.BlockSpec(memory_space=pltpu.VMEM)
        after, velocity = pl.pallas_call(
            functools.partial(kernel, nq),
            out_shape=(
                jax.ShapeDtypeStruct((16, ROWS), F32),
                jax.ShapeDtypeStruct((STEPS, 16, ROWS), F32),
            ),
            in_specs=[pl.BlockSpec(memory_space=pltpu.SMEM)] + [vmem] * 5 + [pl.BlockSpec(memory_space=pl.ANY)],
            out_specs=(vmem, vmem),
            scratch_shapes=[
                pltpu.VMEM((16, SPACE, ROWS, D), BF16),
                pltpu.VMEM((3, 3, ROWS, D), BF16),
                pltpu.VMEM((STEPS, SPACE, 16, ROWS), BF16),
                pltpu.VMEM((STEPS, 16, ROWS), F32),
                pltpu.VMEM((16, ROWS), F32),
                pltpu.VMEM((SPACE, 1, 2 * D), F32),
                pltpu.VMEM((8, 2 * D), F32),
                pltpu.VMEM((1, 2 * D), F32),
                pltpu.VMEM((6, 1, D), F32),
                pltpu.VMEM((SPACE, ROWS, D), BF16),
                pltpu.VMEM((SPACE * ROWS, 144), BF16),
                pltpu.VMEM((SPACE * ROWS, 144), BF16),
                pltpu.VMEM((SPACE * ROWS, 144), BF16),
                pltpu.VMEM((STEPS, SPACE, ROWS, 144), BF16),
                pltpu.VMEM((STEPS, SPACE, ROWS, 144), BF16),
                pltpu.VMEM((ROWS, D), F32),
                pltpu.VMEM((STEPS, 10, ROWS, D), BF16),
                pltpu.VMEM((3, ROWS, THIRD), BF16),
                pltpu.VMEM((3, ROWS, THIRD), BF16),
                pltpu.VMEM((SLOTS, ROWS, 128), F32),
                pltpu.VMEM((3, SLOTS, ROWS, THIRD), BF16),
                pltpu.VMEM((3, THIRD, 128), BF16),
                pltpu.VMEM((3, 128, THIRD), BF16),
                pltpu.VMEM((2, 16, ROWS), BF16),
                pltpu.VMEM((STEPS, 16, ROWS), F32),
                dma((6,)),
                dma((7,)), dma((SPACE,)),
                dma((7,)), dma((SPACE,)),
                dma((ROUNDS,)), dma((ROUNDS,)),
                dma((ROUNDS, 2, 2)), dma((ROUNDS, 2, 2)),
                dma((ROUNDS, 2)), dma((ROUNDS, 2)),
                dma((ROUNDS, 5)), dma((ROUNDS, 5)),
                dma((ROUNDS, 10)), dma((ROUNDS, 10)),
                dma((STEPS, 7)), dma((STEPS, SPACE)),
                dma((STEPS, 4)), dma((STEPS, 4)),
                dma((STEPS, 5)), dma((STEPS, 5)),
                dma((2, SPACE)), dma((SPACE,)),
                dma((STEPS,)), dma((STEPS,)),
            ],
            compiler_params=pltpu.CompilerParams(
                collective_id=0, has_side_effects=True, vmem_limit_bytes=56 << 20
            ),
            name="denoise",
        )(
            levels, latents[0].T, jnp.swapaxes(fresh_noise, 1, 2), modulation_weight.T, embed_weight,
            final_weight.T, attention_weights.reshape(8, 3, ROWS, D),
        )
        return after.T[None], jnp.swapaxes(velocity, 1, 2)[:, None]

    in_specs = (
        P("queue", "space", None),
        P(None, "space", None),
        P(),
        P(None, "space"),
        P(),
        P(None, "space", None),
        P(),
    )
    out_specs = (P("queue", "space", None), P(None, "queue", "space", None))
    return jax.shard_map(local, mesh=mesh, in_specs=in_specs, out_specs=out_specs, check_vma=False)
```

```python
import functools
import math

import jax
import jax.numpy as jnp
from jax import lax
from jax.experimental import pallas as pl
from jax.experimental.pallas import tpu as pltpu
from jax.sharding import PartitionSpec as P

HEAD = 72
FREQ = 256
STEPS = 2
REACH = 4
LEVELS = 1000
D = 1152
ROWS = 48
NX = 4
NY = 8
SPACE = 8
ROUNDS = 4
THIRD = 384
SLOTS = 2 * REACH + 2
SCALE = 1.0 / math.sqrt(HEAD)
MESH = pl.DeviceIdType.MESH
F32 = jnp.float32
BF16 = jnp.bfloat16
SLOT = {(dx, dz): dz * NX + at for dz in range(2) for at, dx in enumerate((0, 3, 1, 2))}
PEERS = [place for place in SLOT if place != (0, 0)]
PARTS = [(1, 2), (3, 1), (4, 1), (5, 2), (7, 1)]
OVER_Z = (2, 4)
CHIPS = [-2, -1, 1, 2]


def time_features(level):
    half_size = FREQ // 2
    places = lax.broadcasted_iota(jnp.int32, (8, half_size), 1).astype(F32)
    frequency = jnp.exp(-math.log(10000.0) * places / half_size)
    angles = (level.astype(F32) / LEVELS * 1000.0) * frequency
    return jnp.concatenate([jnp.cos(angles), jnp.sin(angles)], -1).astype(BF16)


def layer_norm(values):
    average = jnp.mean(values, -1, keepdims=True)
    centred = values - average
    variance = jnp.mean(centred * centred, -1, keepdims=True)
    return centred * lax.rsqrt(variance + 1e-06)


def dot(a, b):
    return lax.dot_general(a, b, (((1,), (0,)), ((), ())), preferred_element_type=F32)


def t_dot(a, b):
    return lax.dot_general(a, b, (((0,), (0,)), ((), ())), preferred_element_type=F32)


def dot_t(a, b):
    return lax.dot_general(a, b, (((1,), (1,)), ((), ())), preferred_element_type=F32)


def kernel(
    nq,
    levels, lat, fresh, mw, emb, fin, aw,
    after, velocity,
    wf, ws, tok, zf, zcur, mods, mstage, mline, mvec, n1s, qs, ks, vs, a1s, a1r,
    h1s, n2b, q2s, a2s, sc, v2s, hm, hmt, ub, us,
    lsem, lat_s, lat_r, mod_s, mod_r, w_s, z_r, x_r, f_r, y_r, c_r,
    a_s, a_r, n_s, n_r, b_s, b_r, u_s, u_r, v_s, v_r,
):
    q = lax.axis_index("queue")
    s = lax.axis_index("space")
    x, zh = lax.div(s, 2), lax.rem(s, 2)
    chip, core = lax.div(q, 2), lax.rem(q, 2)
    line, y = lax.div(chip, NY), lax.rem(chip, NY)
    parity = lax.rem(y + line, 2)
    chips = nq // 2

    def peer(dx, dz):
        return lax.rem(x + dx, NX) * 2 + lax.rem(zh + dz, 2)

    def along_y(by):
        return (line * NY + lax.rem(y + by + NY, NY)) * 2 + core

    sibling = chip * 2 + 1 - core
    lines = nq // (2 * NY)
    mirror = ((lines - 1 - line) * NY + y) * 2 + core
    beside = ((line + 1 - 2 * lax.rem(line, 2)) * NY + y) * 2 + core
    ahead, behind = along_y(1 - 2 * core), along_y(2 * core - 1)
    sends = []

    def remote(src, dst, ss, rs, to_q, to_s):
        return pltpu.make_async_remote_copy(
            src_ref=src, dst_ref=dst, send_sem=ss, recv_sem=rs,
            device_id=(to_q, to_s), device_id_type=MESH,
        )

    def send(src, dst, ss, rs, to_q, to_s, when=None, grouped=False):
        copy = remote(src, dst, ss, rs, to_q, to_s)
        if when is None:
            copy.start()
        else:
            pl.when(when)(copy.start)
        if not grouped:
            sends.append((copy, when))

    def left(src, ss, when=None):
        sends.append((remote(src, src, ss, ss, q, s), when))

    def arrived(dst, rs, when=None):
        copy = remote(dst, dst, rs, rs, q, s)
        if when is None:
            copy.wait_recv()
        else:
            pl.when(when)(copy.wait_recv)

    loads = [pltpu.make_async_copy(aw.at[pl.ds(0, 3)], ws, lsem.at[5])]
    for m in range(5):
        loads.append(
            pltpu.make_async_copy(aw.at[3 + m], wf.at[pl.ds(3 * m, 3), 0], lsem.at[m])
        )
    for load in loads[1:]:
        load.start()
    loads[0].start()

    barrier = pltpu.get_barrier_semaphore()

    def signal(to_q, to_s):
        pl.semaphore_signal(barrier, inc=1, device_id=(to_q, to_s), device_id_type=MESH)

    for dx, dz in PEERS:
        signal(q, peer(dx, dz))
    signal(behind, s)
    signal(beside, s)
    signal(sibling, s)
    signal(mirror, peer(0, 1))
    expected = len(PEERS) + 4
    for dc in (-1, 1):
        there = (chip + dc >= 0) & (chip + dc < chips)

        @pl.when(there)
        def _(dc=dc):
            signal((chip + dc) * 2 + core, s)

        expected = expected + there.astype(jnp.int32)

    @pl.when(q < nq - 1)
    def _():
        for dx in range(NX):
            for dz in range(2):
                signal(q + 1, peer(dx, dz))

    expected = expected + jnp.where(q > 0, SPACE, 0)

    tok[0, 0] = lat[...].astype(BF16)
    zcur[...] = lat[...]
    wf[15, 0] = jnp.zeros((ROWS, D), BF16)
    mstage[...] = jnp.zeros_like(mstage)
    mstage[:, 0:864] = dot_t(time_features(levels[q]), mw[...])
    shift = lax.rem(s * 864, D)
    mline[...] = pltpu.roll(mstage[...], shift, 1)[0:1, :]
    for t in range(3):
        for ref, (row, lane) in ((hm, (0, 1)), (hmt, (1, 0))):
            shape = ref.shape[1:]
            place = lax.broadcasted_iota(jnp.int32, shape, row)
            head = lax.broadcasted_iota(jnp.int32, shape, lane)
            at = place - (head >> 1) * ROWS
            second = (at + t * ROWS >= HEAD).astype(jnp.int32)
            ref[t] = jnp.where((at >= 0) & (at < ROWS) & (second == (head & 1)), 1.0, 0.0).astype(BF16)
    for step in range(STEPS):
        n2b[step, 9 - 9 * core] = jnp.zeros((ROWS, D), BF16)
    for dc in CHIPS:
        @pl.when((chip + dc < 0) | (chip + dc >= chips))
        def _(dc=dc):
            for step in range(STEPS):
                for c in range(2):
                    n2b[step, (dc + 2) * 2 + c] = jnp.zeros((ROWS, D), BF16)

    pl.semaphore_wait(barrier, expected)

    for i, (dx, dz) in enumerate(PEERS):
        back = SLOT[-dx % NX, dz]
        send(tok.at[0, 0], tok.at[0, back], lat_s.at[0], lat_r.at[0], q, peer(dx, dz), grouped=True)
    left(tok.at[0, 0:7], lat_s.at[0])
    for i, (dx, dz) in enumerate(PEERS):
        back = SLOT[-dx % NX, dz]
        send(mline, mods.at[s], mod_s.at[0], mod_r.at[0], q, peer(dx, dz), grouped=True)
    left(mods.at[0:7], mod_s.at[0])
    mods[s] = mline[...]

    def chunk(i, p, c):
        return 4 * i + 2 * p + c

    def own_out(i):
        j = chunk(i, parity, core)
        send(wf.at[j, 0], wf.at[j, 1], w_s.at[0], x_r.at[i, 0, 0], q, peer(1, 0), grouped=True)
        send(wf.at[j, 0], wf.at[j, 2], w_s.at[0], x_r.at[i, 0, 1], q, peer(3, 0), grouped=True)

    def cross_out(i):
        j = chunk(i, 1 - parity, core)
        send(wf.at[j, 0], wf.at[j, 4], w_s.at[0], z_r.at[i], mirror, peer(0, 1), grouped=True)

    def share(i, part):
        j = chunk(i, parity, core)
        at = pl.ds(*PARTS[part])
        to = beside if part in OVER_Z else ahead
        send(wf.at[j, at], wf.at[j, at], w_s.at[0], y_r.at[i, part], to, s, grouped=True)
        send(wf.at[j, at], wf.at[j, at], w_s.at[1], c_r.at[i, 0], sibling, s, grouped=True)

    def onward(i, half):
        j = chunk(i, parity, core)
        base = 4 * half
        arrived(wf.at[j, base + 1], x_r.at[i, half, 0])
        arrived(wf.at[j, base + 2], x_r.at[i, half, 1])
        to = lax.rem(x + 1 + 2 * core, NX) * 2 + zh
        send(wf.at[j, base + 1 + core], wf.at[j, base + 3], w_s.at[0], f_r.at[i, half], q, to, grouped=True)
        share(i, 3 * half)

    def far_in(i, half):
        j = chunk(i, parity, core)
        arrived(wf.at[j, 4 * half + 3], f_r.at[i, half])
        share(i, 3 * half + 1)

    def cross_in(i):
        j = chunk(i, parity, core)
        arrived(wf.at[j, 4], z_r.at[i])
        send(wf.at[j, 4], wf.at[j, 5], w_s.at[0], x_r.at[i, 1, 0], q, peer(1, 0), grouped=True)
        send(wf.at[j, 4], wf.at[j, 6], w_s.at[0], x_r.at[i, 1, 1], q, peer(3, 0), grouped=True)
        share(i, 2)

    def pass_on(i, *parts):
        j = chunk(i, 1 - parity, core)
        for part in parts:
            at = pl.ds(*PARTS[part])
            arrived(wf.at[j, at], y_r.at[i, part])
            send(wf.at[j, at], wf.at[j, at], w_s.at[1], c_r.at[i, 1], sibling, s, grouped=True)

    def complete(i):
        for half, p in ((0, parity), (1, 1 - parity)):
            arrived(wf.at[chunk(i, p, 1 - core), 1:8], c_r.at[i, half])

    for group in range(2):
        left(wf.at[0:7], w_s.at[group])

    for load in loads[1:]:
        load.wait()
    for i in range(ROUNDS):
        own_out(i)
    cross_out(0)

    arrived(mods.at[0:7], mod_r.at[0])
    for base in (0, 4):
        piece = base // 4 * 3
        lower = [mods[base + g][:, 0:D] for g in range(4)]
        upper = [mods[base + g][:, D : 2 * D] for g in range(4)]
        mvec[piece] = lower[0] + lower[1]
        mvec[piece + 1] = upper[1] + lower[2]
        mvec[piece + 2] = upper[2] + lower[3]

    loads[0].wait()
    lane = lax.broadcasted_iota(jnp.int32, (1, 144), 1)
    in_first = lane < HEAD
    pick = (
        lax.broadcasted_iota(jnp.int32, (16, 144), 1)
        == lax.broadcasted_iota(jnp.int32, (16, 144), 0) + 128
    ).astype(F32).astype(BF16)

    def embed(step, *slots):
        for r in slots:
            if step == 0:
                if r == 1:
                    arrived(tok.at[0, 1:8], lat_r.at[0])
            elif r in (1, 4):
                arrived(tok.at[step, r : 4 if r == 1 else SPACE], u_r.at[r // 4 + 1])
            elif r == 0:
                arrived(tok.at[step, 0], u_r.at[0], q < nq - 1)

                @pl.when(q == nq - 1)
                def _():
                    tok[step, 0] = fresh[step - 1].astype(BF16)

            h0 = t_dot(tok[step, r], emb[...])
            n1s[r] = (layer_norm(h0) * (1.0 + mvec[1]) + mvec[0]).astype(BF16)

    def project(*indices):
        for index in indices:
            (qs, ks, vs)[index][...] = dot_t(
                n1s[...].reshape(SPACE * ROWS, D), ws[index].reshape(144, D)
            ).astype(BF16)

    def attend(step, b):
        query = qs[b * 96 : b * 96 + 96, :]
        heads = []
        for h in range(2):
            mine = in_first if h == 0 else ~in_first
            scores = dot_t(jnp.where(mine, query, jnp.zeros_like(query)), ks[...]) * SCALE
            e = jnp.exp(scores - jnp.max(scores, -1, keepdims=True))
            p = (e * (1.0 / jnp.sum(e, -1, keepdims=True))).astype(BF16)
            heads.append(dot(p, vs[...]))
        a1 = jnp.where(in_first, heads[0], heads[1]).astype(BF16)
        a1s[step, 2 * b : 2 * b + 2, 0:3] = a1[:, 0:128].reshape(2, 3, 16, 128)
        for half in range(2):
            rest = dot_t(pick, a1[half * ROWS : half * ROWS + ROWS])
            a1s[step, 2 * b + half, 3, :, 0:ROWS] = rest.astype(BF16)
        for i, (dx, dz) in enumerate(PEERS):
            if SLOT[dx, dz] // 2 == b:
                back = SLOT[-dx % NX, dz]
                send(a1s.at[step, SLOT[dx, dz]], a1r.at[step, back],
                     a_s.at[step], a_r.at[step, back // 4], q, peer(dx, dz), grouped=True)
        if b == 0:
            a1r[step, 0] = a1s[step, 0]
            left(a1s.at[step, 0:7], a_s.at[step])

    def middle(step):
        h0 = t_dot(tok[step, 0], emb[...])
        o1 = jnp.zeros((ROWS, D), F32)
        for r in range(SPACE):
            if r in (1, 4):
                arrived(a1r.at[step, r : 4 if r == 1 else SPACE], a_r.at[step, r // 4])
            top = wf[0:3, r].reshape(144, D)[0:128]
            o1 = o1 + dot(a1r[step, r, 0:3].reshape(ROWS, 128), top)
        rest = jnp.concatenate([a1r[step, r, 3, :, 0:ROWS] for r in range(SPACE)], 0)
        bottom = wf[2, :, 32:ROWS].reshape(128, D)
        o1 = o1 + t_dot(rest, bottom)
        h1 = h0 + mvec[2] * o1
        h1s[...] = h1
        n2 = layer_norm(h1) * (1.0 + mvec[4]) + mvec[3]
        n2b[step, 4 + core] = n2.astype(BF16)
        own = n2b.at[step, 4 + core]
        send(own, own, b_s.at[step, 4], b_r.at[step, 4], sibling, s)
        for i in (1, 2):
            dc = CHIPS[i]
            there = (chip + dc >= 0) & (chip + dc < chips)
            send(own, n2b.at[step, (2 - dc) * 2 + core], n_s.at[step, i], n_r.at[step, 3 - i],
                 (chip + dc) * 2 + core, s, there)

    def relay(step, *chips_from):
        for i in chips_from:
            dc = CHIPS[i]
            there = (chip + dc >= 0) & (chip + dc < chips)
            slot = (dc + 2) * 2 + core
            arrived(n2b.at[step, slot], n_r.at[step, i], there)
            if i in (1, 2):
                send(n2b.at[step, slot], n2b.at[step, (2 + 2 * dc) * 2 + core], n_s.at[step, 3 * (i - 1)],
                     n_r.at[step, 3 * (i - 1)], (chip - dc) * 2 + core, s,
                     there & (chip - dc >= 0) & (chip - dc < chips))
            wanted = there
            if dc == -2:
                wanted = there & (core == 1)
            if dc == 2:
                wanted = there & (core == 0)
            send(n2b.at[step, slot], n2b.at[step, slot], b_s.at[step, i], b_r.at[step, i],
                 sibling, s, wanted)

    def relayed(step, *chips_from):
        for i in chips_from:
            dc = CHIPS[i]
            there = (chip + dc >= 0) & (chip + dc < chips)
            slot = (dc + 2) * 2 + 1 - core
            wanted = there
            if dc == -2:
                wanted = there & (core == 0)
            if dc == 2:
                wanted = there & (core == 1)
            arrived(n2b.at[step, slot], b_r.at[step, i], wanted)

    def queries(step):
        for t in range(3):
            q2s[t] = dot_t(n2b[step, 4 + core], wf[3 + t].reshape(THIRD, D)).astype(BF16)
        arrived(n2b.at[step, 5 - core], b_r.at[step, 4])

    def rows_of(step, groups):
        blocks = [n2b[step, low:high] for low, high in groups]
        blocks = blocks[0] if len(blocks) == 1 else jnp.concatenate(blocks, 0)
        return blocks.shape[0], blocks.reshape(-1, D)

    def keys(step, *groups):
        count, rows = rows_of(step, groups)
        total = jnp.zeros((count * ROWS, 128), F32)
        for t in range(3):
            k2 = dot_t(rows, wf[6 + t].reshape(THIRD, D)).astype(BF16)
            product = k2.reshape(count, ROWS, THIRD).astype(F32) * q2s[t].astype(F32)[None]
            total = total + dot(product.astype(BF16).reshape(count * ROWS, THIRD), hm[t])
        total = total.reshape(count, ROWS, 128)
        at = 0
        for low, high in groups:
            sc[low:high] = total[at : at + high - low]
            at += high - low

    def values(step, *groups):
        count, rows = rows_of(step, groups)
        for t in range(3):
            v2 = dot_t(rows, wf[9 + t].reshape(THIRD, D)).astype(BF16).reshape(count, ROWS, THIRD)
            at = 0
            for low, high in groups:
                v2s[t, low:high] = v2[at : at + high - low]
                at += high - low

    def blend():
        scores = sc[...] * SCALE
        block = lax.broadcasted_iota(jnp.int32, scores.shape, 0) + 2 * chip - REACH
        usable = (block >= 0) & (block < nq) & (block >= q - REACH) & (block <= q + REACH)
        scores = jnp.where(usable, scores, -1e30)
        e = jnp.exp(scores - jnp.max(scores, 0, keepdims=True))
        p = (e * (1.0 / jnp.sum(e, 0, keepdims=True))).astype(BF16).reshape(SLOTS * ROWS, 128)
        for t in range(3):
            spread = dot(p, hmt[t]).reshape(SLOTS, ROWS, THIRD)
            a2s[t] = jnp.sum(spread * v2s[t].astype(F32), 0).astype(BF16)

    def final(step):
        o2 = dot(a2s[0], wf[12].reshape(THIRD, D))
        for t in range(1, 3):
            o2 = o2 + dot(a2s[t], wf[12 + t].reshape(THIRD, D))
        h2 = h1s[...] + mvec[5] * o2
        v = dot_t(fin[...], layer_norm(h2).astype(BF16))
        velocity[step] = v
        below = jnp.where(q > 0, levels[jnp.maximum(q - 1, 0)], 0)
        u = zcur[...] + ((below - levels[q]).astype(F32) / LEVELS) * v
        us[step] = u
        head = q > 0
        tail = q == nq - 1
        if step < STEPS - 1:
            ub[0] = u.astype(BF16)
            ub[1] = fresh[step].astype(BF16)
            for dx in range(NX):
                for dz in range(2):
                    back = SLOT[-dx % NX, dz]
                    here = SLOT[dx, dz]
                    send(ub.at[0], tok.at[step + 1, back], u_s.at[0], u_r.at[(back > 0) + back // 4],
                         q - 1, peer(dx, dz), head, grouped=True)
                    if here:
                        send(ub.at[1], tok.at[step + 1, back], u_s.at[1], u_r.at[(back > 0) + back // 4],
                             q, peer(dx, dz), tail, grouped=True)
            left(tok.at[0, 0:8], u_s.at[0], head)
            left(tok.at[0, 0:7], u_s.at[1], tail)
        send(us.at[step], zf.at[step], v_s.at[step], v_r.at[step], q - 1, s, head)

    def arrive(step):
        arrived(zf.at[step], v_r.at[step], q < nq - 1)

        @pl.when(q == nq - 1)
        def _():
            zf[step] = fresh[step]

    embed(0, 0, 1, 2, 3)
    onward(0, 0)
    cross_out(1)
    embed(0, 4, 5, 6, 7)
    onward(1, 0)
    project(0)
    cross_in(0)
    cross_out(2)
    pass_on(0, 0)
    project(1, 2)
    onward(2, 0)
    attend(0, 2)
    pass_on(1, 0)
    onward(3, 0)
    attend(0, 3)
    pass_on(0, 2)
    far_in(0, 0)
    cross_in(1)
    cross_out(3)
    attend(0, 1)
    pass_on(2, 0)
    far_in(1, 0)
    pass_on(3, 0)
    attend(0, 0)
    onward(0, 1)
    pass_on(0, 1)
    pass_on(1, 2)
    far_in(2, 0)
    cross_in(2)
    pass_on(1, 1)
    far_in(3, 0)
    pass_on(0, 3)
    onward(1, 1)
    pass_on(2, 1)
    pass_on(2, 2)
    far_in(0, 1)
    cross_in(3)
    pass_on(3, 1)
    onward(2, 1)
    pass_on(1, 3)
    far_in(1, 1)
    pass_on(0, 4)
    complete(0)
    middle(0)
    onward(3, 1)
    pass_on(2, 3)
    pass_on(3, 2)
    far_in(2, 1)
    far_in(3, 1)
    pass_on(1, 4)
    complete(1)
    queries(0)
    relay(0, 1, 2)
    pass_on(3, 3)
    pass_on(2, 4)
    relay(0, 0, 3)
    pass_on(3, 4)
    complete(2)
    relayed(0, 1, 2, 0, 3)
    keys(0, (0, 10))
    values(0, (0, 10))
    blend()
    complete(3)
    final(0)
    embed(1, 0, 1, 2, 3, 4, 5, 6, 7)
    project(0, 1, 2)
    attend(1, 2)
    attend(1, 3)
    attend(1, 1)
    attend(1, 0)
    arrive(0)
    zcur[...] = zf[0]
    middle(1)
    queries(1)
    keys(1, (4, 6))
    values(1, (4, 6))
    relay(1, 1, 2)
    relayed(1, 1, 2)
    keys(1, (2, 4), (6, 8))
    values(1, (2, 4), (6, 8))
    relay(1, 0, 3)
    relayed(1, 0, 3)
    keys(1, (0, 2), (8, 10))
    values(1, (0, 2), (8, 10))
    blend()
    final(1)
    arrive(1)
    after[...] = zf[1]

    for copy, when in sends:
        if when is None:
            copy.wait_send()
        else:
            pl.when(when)(copy.wait_send)


def hand_out(after_in, velocity_in, after, velocity):
    after[...] = after_in[...]
    velocity[...] = velocity_in[...]


def solution(mesh):
    nq = mesh.shape["queue"]

    def local(latents, fresh_noise, levels, modulation_weight, embed_weight, attention_weights, final_weight):
        dma = pltpu.SemaphoreType.DMA
        vmem = pl.BlockSpec(memory_space=pltpu.VMEM)
        after, velocity = pl.pallas_call(
            functools.partial(kernel, nq),
            out_shape=(
                jax.ShapeDtypeStruct((16, ROWS), F32),
                jax.ShapeDtypeStruct((STEPS, 16, ROWS), F32),
            ),
            in_specs=[pl.BlockSpec(memory_space=pltpu.SMEM)] + [vmem] * 5 + [pl.BlockSpec(memory_space=pl.ANY)],
            out_specs=(vmem, vmem),
            scratch_shapes=[
                pltpu.VMEM((16, SPACE, ROWS, D), BF16),
                pltpu.VMEM((3, 3, ROWS, D), BF16),
                pltpu.VMEM((STEPS, SPACE, 16, ROWS), BF16),
                pltpu.VMEM((STEPS, 16, ROWS), F32),
                pltpu.VMEM((16, ROWS), F32),
                pltpu.VMEM((SPACE, 1, 2 * D), F32),
                pltpu.VMEM((8, 2 * D), F32),
                pltpu.VMEM((1, 2 * D), F32),
                pltpu.VMEM((6, 1, D), F32),
                pltpu.VMEM((SPACE, ROWS, D), BF16),
                pltpu.VMEM((SPACE * ROWS, 144), BF16),
                pltpu.VMEM((SPACE * ROWS, 144), BF16),
                pltpu.VMEM((SPACE * ROWS, 144), BF16),
                pltpu.VMEM((STEPS, SPACE, 4, 16, 128), BF16),
                pltpu.VMEM((STEPS, SPACE, 4, 16, 128), BF16),
                pltpu.VMEM((ROWS, D), F32),
                pltpu.VMEM((STEPS, 10, ROWS, D), BF16),
                pltpu.VMEM((3, ROWS, THIRD), BF16),
                pltpu.VMEM((3, ROWS, THIRD), BF16),
                pltpu.VMEM((SLOTS, ROWS, 128), F32),
                pltpu.VMEM((3, SLOTS, ROWS, THIRD), BF16),
                pltpu.VMEM((3, THIRD, 128), BF16),
                pltpu.VMEM((3, 128, THIRD), BF16),
                pltpu.VMEM((2, 16, ROWS), BF16),
                pltpu.VMEM((STEPS, 16, ROWS), F32),
                dma((6,)),
                dma((1,)), dma((1,)),
                dma((1,)), dma((1,)),
                dma((2,)), dma((ROUNDS,)), dma((ROUNDS, 2, 2)), dma((ROUNDS, 2)),
                dma((ROUNDS, 5)), dma((ROUNDS, 2)),
                dma((STEPS,)), dma((STEPS, 2)),
                dma((STEPS, 4)), dma((STEPS, 4)),
                dma((STEPS, 5)), dma((STEPS, 5)),
                dma((2,)), dma((3,)),
                dma((STEPS,)), dma((STEPS,)),
            ],
            compiler_params=pltpu.CompilerParams(
                collective_id=0, has_side_effects=True, vmem_limit_bytes=56 << 20
            ),
            name="denoise",
        )(
            levels, latents[0].T, jnp.swapaxes(fresh_noise, 1, 2), modulation_weight.T, embed_weight,
            final_weight.T, attention_weights.reshape(8, 3, ROWS, D),
        )
        after, velocity = pl.pallas_call(
            hand_out, out_shape=(after, velocity), in_specs=[vmem] * 2, out_specs=(vmem, vmem), name="hand_out"
        )(after, velocity)
        return after.T[None], jnp.swapaxes(velocity, 1, 2)[:, None]

    in_specs = (
        P("queue", "space", None),
        P(None, "space", None),
        P(),
        P(None, "space"),
        P(),
        P(None, "space", None),
        P(),
    )
    out_specs = (P("queue", "space", None), P(None, "queue", "space", None))
    return jax.shard_map(local, mesh=mesh, in_specs=in_specs, out_specs=out_specs, check_vma=False)
```

```python
import functools
import math

import jax
import jax.numpy as jnp
from jax import lax
from jax.experimental import pallas as pl
from jax.experimental.pallas import tpu as pltpu
from jax.sharding import PartitionSpec as P

HEAD = 72
FREQ = 256
STEPS = 2
REACH = 4
LEVELS = 1000
D = 1152
ROWS = 48
NX = 4
NY = 8
SPACE = 8
ROUNDS = 4
THIRD = 384
SLOTS = 2 * REACH + 2
SCALE = 1.0 / math.sqrt(HEAD)
MESH = pl.DeviceIdType.MESH
F32 = jnp.float32
BF16 = jnp.bfloat16
SLOT = {(dx, dz): dz * NX + at for dz in range(2) for at, dx in enumerate((0, 3, 1, 2))}
PEERS = [place for place in SLOT if place != (0, 0)]
PARTS = [(1, 2), (3, 1), (4, 1), (5, 2), (7, 1)]
OVER_Z = (2, 4)
CHIPS = [-2, -1, 1, 2]


def time_features(level):
    half_size = FREQ // 2
    places = lax.broadcasted_iota(jnp.int32, (8, half_size), 1).astype(F32)
    frequency = jnp.exp(-math.log(10000.0) * places / half_size)
    angles = (level.astype(F32) / LEVELS * 1000.0) * frequency
    return jnp.concatenate([jnp.cos(angles), jnp.sin(angles)], -1).astype(BF16)


def layer_norm(values):
    average = jnp.mean(values, -1, keepdims=True)
    centred = values - average
    variance = jnp.mean(centred * centred, -1, keepdims=True)
    return centred * lax.rsqrt(variance + 1e-06)


def dot(a, b):
    return lax.dot_general(a, b, (((1,), (0,)), ((), ())), preferred_element_type=F32)


def t_dot(a, b):
    return lax.dot_general(a, b, (((0,), (0,)), ((), ())), preferred_element_type=F32)


def dot_t(a, b):
    return lax.dot_general(a, b, (((1,), (1,)), ((), ())), preferred_element_type=F32)


def kernel(
    nq,
    levels, lat, fresh, mw, emb, fin, aw,
    after, velocity,
    wf, ws, tok, zf, zcur, mods, mstage, mline, mvec, n1s, qs, ks, vs, a1s, a1r,
    h1s, n2b, q2s, a2s, sc, v2s, hm, hmt, ub, us,
    lsem, lat_s, lat_r, mod_s, mod_r, w_s, z_r, x_r, f_r, y_r, c_r,
    a_s, a_r, n_s, n_r, b_s, b_r, u_s, u_r, v_s, v_r,
):
    q = lax.axis_index("queue")
    s = lax.axis_index("space")
    x, zh = lax.div(s, 2), lax.rem(s, 2)
    chip, core = lax.div(q, 2), lax.rem(q, 2)
    line, y = lax.div(chip, NY), lax.rem(chip, NY)
    parity = lax.rem(y + line, 2)
    chips = nq // 2

    def peer(dx, dz):
        return lax.rem(x + dx, NX) * 2 + lax.rem(zh + dz, 2)

    def along_y(by):
        return (line * NY + lax.rem(y + by + NY, NY)) * 2 + core

    sibling = chip * 2 + 1 - core
    lines = nq // (2 * NY)
    mirror = ((lines - 1 - line) * NY + y) * 2 + core
    beside = ((line + 1 - 2 * lax.rem(line, 2)) * NY + y) * 2 + core
    ahead, behind = along_y(1 - 2 * core), along_y(2 * core - 1)
    sends = []

    def remote(src, dst, ss, rs, to_q, to_s):
        return pltpu.make_async_remote_copy(
            src_ref=src, dst_ref=dst, send_sem=ss, recv_sem=rs,
            device_id=(to_q, to_s), device_id_type=MESH,
        )

    def send(src, dst, ss, rs, to_q, to_s, when=None, grouped=False):
        copy = remote(src, dst, ss, rs, to_q, to_s)
        if when is None:
            copy.start()
        else:
            pl.when(when)(copy.start)
        if not grouped:
            sends.append((copy, when))

    def left(src, ss, when=None):
        sends.append((remote(src, src, ss, ss, q, s), when))

    def arrived(dst, rs, when=None):
        copy = remote(dst, dst, rs, rs, q, s)
        if when is None:
            copy.wait_recv()
        else:
            pl.when(when)(copy.wait_recv)

    loads = [pltpu.make_async_copy(aw.at[pl.ds(0, 3)], ws, lsem.at[5])]
    for m in range(5):
        loads.append(
            pltpu.make_async_copy(aw.at[3 + m], wf.at[pl.ds(3 * m, 3), 0], lsem.at[m])
        )
    for load in loads[1:]:
        load.start()
    loads[0].start()

    barrier = pltpu.get_barrier_semaphore()

    def signal(to_q, to_s):
        pl.semaphore_signal(barrier, inc=1, device_id=(to_q, to_s), device_id_type=MESH)

    for dx, dz in PEERS:
        signal(q, peer(dx, dz))
    signal(behind, s)
    signal(beside, s)
    signal(sibling, s)
    signal(mirror, peer(0, 1))
    expected = len(PEERS) + 4
    for dc in (-1, 1):
        there = (chip + dc >= 0) & (chip + dc < chips)

        @pl.when(there)
        def _(dc=dc):
            signal((chip + dc) * 2 + core, s)

        expected = expected + there.astype(jnp.int32)

    @pl.when(q < nq - 1)
    def _():
        for dx in range(NX):
            for dz in range(2):
                signal(q + 1, peer(dx, dz))

    expected = expected + jnp.where(q > 0, SPACE, 0)

    tok[0, 0] = lat[...].astype(BF16)
    zcur[...] = lat[...]
    wf[15, 0] = jnp.zeros((ROWS, D), BF16)
    mstage[...] = jnp.zeros_like(mstage)
    mstage[:, 0:864] = dot_t(time_features(levels[q]), mw[...])
    shift = lax.rem(s * 864, D)
    mline[...] = pltpu.roll(mstage[...], shift, 1)[0:1, :]
    for t in range(3):
        for ref, (row, lane) in ((hm, (0, 1)), (hmt, (1, 0))):
            shape = ref.shape[1:]
            place = lax.broadcasted_iota(jnp.int32, shape, row)
            head = lax.broadcasted_iota(jnp.int32, shape, lane)
            at = place - (head >> 1) * ROWS
            second = (at + t * ROWS >= HEAD).astype(jnp.int32)
            ref[t] = jnp.where((at >= 0) & (at < ROWS) & (second == (head & 1)), 1.0, 0.0).astype(BF16)
    for step in range(STEPS):
        n2b[step, 9 - 9 * core] = jnp.zeros((ROWS, D), BF16)
    for dc in CHIPS:
        @pl.when((chip + dc < 0) | (chip + dc >= chips))
        def _(dc=dc):
            for step in range(STEPS):
                for c in range(2):
                    n2b[step, (dc + 2) * 2 + c] = jnp.zeros((ROWS, D), BF16)

    pl.semaphore_wait(barrier, expected)

    for i, (dx, dz) in enumerate(PEERS):
        back = SLOT[-dx % NX, dz]
        send(tok.at[0, 0], tok.at[0, back], lat_s.at[0], lat_r.at[0], q, peer(dx, dz), grouped=True)
    left(tok.at[0, 0:7], lat_s.at[0])
    for i, (dx, dz) in enumerate(PEERS):
        back = SLOT[-dx % NX, dz]
        send(mline, mods.at[s], mod_s.at[0], mod_r.at[0], q, peer(dx, dz), grouped=True)
    left(mods.at[0:7], mod_s.at[0])
    mods[s] = mline[...]

    def chunk(i, p, c):
        return 4 * i + 2 * p + c

    def own_out(i):
        j = chunk(i, parity, core)
        send(wf.at[j, 0], wf.at[j, 1], w_s.at[0], x_r.at[i, 0, 0], q, peer(1, 0), grouped=True)
        send(wf.at[j, 0], wf.at[j, 2], w_s.at[0], x_r.at[i, 0, 1], q, peer(3, 0), grouped=True)

    def cross_out(i):
        j = chunk(i, 1 - parity, core)
        send(wf.at[j, 0], wf.at[j, 4], w_s.at[0], z_r.at[i], mirror, peer(0, 1), grouped=True)

    def share(i, part):
        j = chunk(i, parity, core)
        at = pl.ds(*PARTS[part])
        to = beside if part in OVER_Z else ahead
        send(wf.at[j, at], wf.at[j, at], w_s.at[0], y_r.at[i, part], to, s, grouped=True)
        send(wf.at[j, at], wf.at[j, at], w_s.at[1], c_r.at[i, 0], sibling, s, grouped=True)

    def onward(i, half):
        j = chunk(i, parity, core)
        base = 4 * half
        arrived(wf.at[j, base + 1], x_r.at[i, half, 0])
        arrived(wf.at[j, base + 2], x_r.at[i, half, 1])
        to = lax.rem(x + 1 + 2 * core, NX) * 2 + zh
        send(wf.at[j, base + 1 + core], wf.at[j, base + 3], w_s.at[0], f_r.at[i, half], q, to, grouped=True)
        share(i, 3 * half)

    def far_in(i, half):
        j = chunk(i, parity, core)
        arrived(wf.at[j, 4 * half + 3], f_r.at[i, half])
        share(i, 3 * half + 1)

    def cross_in(i):
        j = chunk(i, parity, core)
        arrived(wf.at[j, 4], z_r.at[i])
        send(wf.at[j, 4], wf.at[j, 5], w_s.at[0], x_r.at[i, 1, 0], q, peer(1, 0), grouped=True)
        send(wf.at[j, 4], wf.at[j, 6], w_s.at[0], x_r.at[i, 1, 1], q, peer(3, 0), grouped=True)
        share(i, 2)

    def pass_on(i, *parts):
        j = chunk(i, 1 - parity, core)
        for part in parts:
            at = pl.ds(*PARTS[part])
            arrived(wf.at[j, at], y_r.at[i, part])
            send(wf.at[j, at], wf.at[j, at], w_s.at[1], c_r.at[i, 1], sibling, s, grouped=True)

    def complete(i):
        for half, p in ((0, parity), (1, 1 - parity)):
            arrived(wf.at[chunk(i, p, 1 - core), 1:8], c_r.at[i, half])

    for group in range(2):
        left(wf.at[0:7], w_s.at[group])

    for load in loads[1:]:
        load.wait()
    for i in range(ROUNDS):
        own_out(i)
    cross_out(0)

    arrived(mods.at[0:7], mod_r.at[0])
    for base in (0, 4):
        piece = base // 4 * 3
        lower = [mods[base + g][:, 0:D] for g in range(4)]
        upper = [mods[base + g][:, D : 2 * D] for g in range(4)]
        mvec[piece] = lower[0] + lower[1]
        mvec[piece + 1] = upper[1] + lower[2]
        mvec[piece + 2] = upper[2] + lower[3]

    loads[0].wait()
    lane = lax.broadcasted_iota(jnp.int32, (1, 144), 1)
    in_first = lane < HEAD
    pick = (
        lax.broadcasted_iota(jnp.int32, (16, 144), 1)
        == lax.broadcasted_iota(jnp.int32, (16, 144), 0) + 128
    ).astype(F32).astype(BF16)

    def embed(step, *slots):
        for r in slots:
            if step == 0:
                if r == 1:
                    arrived(tok.at[0, 1:8], lat_r.at[0])
            elif r in (1, 4):
                arrived(tok.at[step, r : 4 if r == 1 else SPACE], u_r.at[r // 4 + 1])
            elif r == 0:
                arrived(tok.at[step, 0], u_r.at[0], q < nq - 1)

                @pl.when(q == nq - 1)
                def _():
                    tok[step, 0] = fresh[step - 1].astype(BF16)

        low, count = slots[0], len(slots)
        h0 = jnp.concatenate([t_dot(tok[step, r], emb[...]) for r in slots], 0)
        n1 = (layer_norm(h0) * (1.0 + mvec[1]) + mvec[0]).astype(BF16)
        n1s[low : low + count] = n1.reshape(count, ROWS, D)

    def project(*indices):
        for index in indices:
            (qs, ks, vs)[index][...] = dot_t(
                n1s[...].reshape(SPACE * ROWS, D), ws[index].reshape(144, D)
            ).astype(BF16)

    def attend(step, b):
        query = qs[b * 192 : b * 192 + 192, :]
        heads = []
        for h in range(2):
            mine = in_first if h == 0 else ~in_first
            scores = dot_t(jnp.where(mine, query, jnp.zeros_like(query)), ks[...]) * SCALE
            e = jnp.exp(scores - jnp.max(scores, -1, keepdims=True))
            p = (e * (1.0 / jnp.sum(e, -1, keepdims=True))).astype(BF16)
            heads.append(dot(p, vs[...]))
        a1 = jnp.where(in_first, heads[0], heads[1]).astype(BF16)
        a1s[step, 4 * b : 4 * b + 4, 0:3] = a1[:, 0:128].reshape(4, 3, 16, 128)
        for part in range(4):
            rest = dot_t(pick, a1[part * ROWS : part * ROWS + ROWS])
            a1s[step, 4 * b + part, 3, :, 0:ROWS] = rest.astype(BF16)
        for i, (dx, dz) in enumerate(PEERS):
            if SLOT[dx, dz] // 4 == b:
                back = SLOT[-dx % NX, dz]
                send(a1s.at[step, SLOT[dx, dz]], a1r.at[step, back],
                     a_s.at[step], a_r.at[step, back // 4], q, peer(dx, dz), grouped=True)
        if b == 0:
            a1r[step, 0] = a1s[step, 0]
            left(a1s.at[step, 0:7], a_s.at[step])

    def middle(step):
        h0 = t_dot(tok[step, 0], emb[...])
        o1 = jnp.zeros((ROWS, D), F32)
        for r in range(SPACE):
            if r in (1, 4):
                arrived(a1r.at[step, r : 4 if r == 1 else SPACE], a_r.at[step, r // 4])
            top = wf[0:3, r].reshape(144, D)[0:128]
            o1 = o1 + dot(a1r[step, r, 0:3].reshape(ROWS, 128), top)
        rest = jnp.concatenate([a1r[step, r, 3, :, 0:ROWS] for r in range(SPACE)], 0)
        bottom = wf[2, :, 32:ROWS].reshape(128, D)
        o1 = o1 + t_dot(rest, bottom)
        h1 = h0 + mvec[2] * o1
        h1s[...] = h1
        n2 = layer_norm(h1) * (1.0 + mvec[4]) + mvec[3]
        n2b[step, 4 + core] = n2.astype(BF16)
        own = n2b.at[step, 4 + core]
        send(own, own, b_s.at[step, 4], b_r.at[step, 4], sibling, s)
        for i in (1, 2):
            dc = CHIPS[i]
            there = (chip + dc >= 0) & (chip + dc < chips)
            send(own, n2b.at[step, (2 - dc) * 2 + core], n_s.at[step, i], n_r.at[step, 3 - i],
                 (chip + dc) * 2 + core, s, there)

    def relay(step, *chips_from):
        for i in chips_from:
            dc = CHIPS[i]
            there = (chip + dc >= 0) & (chip + dc < chips)
            slot = (dc + 2) * 2 + core
            arrived(n2b.at[step, slot], n_r.at[step, i], there)
            if i in (1, 2):
                send(n2b.at[step, slot], n2b.at[step, (2 + 2 * dc) * 2 + core], n_s.at[step, 3 * (i - 1)],
                     n_r.at[step, 3 * (i - 1)], (chip - dc) * 2 + core, s,
                     there & (chip - dc >= 0) & (chip - dc < chips))
            wanted = there
            if dc == -2:
                wanted = there & (core == 1)
            if dc == 2:
                wanted = there & (core == 0)
            send(n2b.at[step, slot], n2b.at[step, slot], b_s.at[step, i], b_r.at[step, i],
                 sibling, s, wanted)

    def relayed(step, *chips_from):
        for i in chips_from:
            dc = CHIPS[i]
            there = (chip + dc >= 0) & (chip + dc < chips)
            slot = (dc + 2) * 2 + 1 - core
            wanted = there
            if dc == -2:
                wanted = there & (core == 0)
            if dc == 2:
                wanted = there & (core == 1)
            arrived(n2b.at[step, slot], b_r.at[step, i], wanted)

    def queries(step):
        for t in range(3):
            q2s[t] = dot_t(n2b[step, 4 + core], wf[3 + t].reshape(THIRD, D)).astype(BF16)
        arrived(n2b.at[step, 5 - core], b_r.at[step, 4])

    def rows_of(step, groups):
        blocks = [n2b[step, low:high] for low, high in groups]
        blocks = blocks[0] if len(blocks) == 1 else jnp.concatenate(blocks, 0)
        return blocks.shape[0], blocks.reshape(-1, D)

    def keys(step, *groups):
        count, rows = rows_of(step, groups)
        total = jnp.zeros((count * ROWS, 128), F32)
        for t in range(3):
            k2 = dot_t(rows, wf[6 + t].reshape(THIRD, D)).astype(BF16)
            product = k2.reshape(count, ROWS, THIRD).astype(F32) * q2s[t].astype(F32)[None]
            total = total + dot(product.astype(BF16).reshape(count * ROWS, THIRD), hm[t])
        total = total.reshape(count, ROWS, 128)
        at = 0
        for low, high in groups:
            sc[low:high] = total[at : at + high - low]
            at += high - low

    def values(step, *groups):
        count, rows = rows_of(step, groups)
        for t in range(3):
            v2 = dot_t(rows, wf[9 + t].reshape(THIRD, D)).astype(BF16).reshape(count, ROWS, THIRD)
            at = 0
            for low, high in groups:
                v2s[t, low:high] = v2[at : at + high - low]
                at += high - low

    def blend():
        scores = sc[...] * SCALE
        block = lax.broadcasted_iota(jnp.int32, scores.shape, 0) + 2 * chip - REACH
        usable = (block >= 0) & (block < nq) & (block >= q - REACH) & (block <= q + REACH)
        scores = jnp.where(usable, scores, -1e30)
        e = jnp.exp(scores - jnp.max(scores, 0, keepdims=True))
        p = (e * (1.0 / jnp.sum(e, 0, keepdims=True))).astype(BF16).reshape(SLOTS * ROWS, 128)
        for t in range(3):
            spread = dot(p, hmt[t]).reshape(SLOTS, ROWS, THIRD)
            a2s[t] = jnp.sum(spread * v2s[t].astype(F32), 0).astype(BF16)

    def final(step):
        o2 = dot(a2s[0], wf[12].reshape(THIRD, D))
        for t in range(1, 3):
            o2 = o2 + dot(a2s[t], wf[12 + t].reshape(THIRD, D))
        h2 = h1s[...] + mvec[5] * o2
        v = dot_t(fin[...], layer_norm(h2).astype(BF16))
        velocity[step] = v
        below = jnp.where(q > 0, levels[jnp.maximum(q - 1, 0)], 0)
        u = zcur[...] + ((below - levels[q]).astype(F32) / LEVELS) * v
        us[step] = u
        head = q > 0
        tail = q == nq - 1
        if step < STEPS - 1:
            ub[0] = u.astype(BF16)
            ub[1] = fresh[step].astype(BF16)
            for dx in range(NX):
                for dz in range(2):
                    back = SLOT[-dx % NX, dz]
                    here = SLOT[dx, dz]
                    send(ub.at[0], tok.at[step + 1, back], u_s.at[0], u_r.at[(back > 0) + back // 4],
                         q - 1, peer(dx, dz), head, grouped=True)
                    if here:
                        send(ub.at[1], tok.at[step + 1, back], u_s.at[1], u_r.at[(back > 0) + back // 4],
                             q, peer(dx, dz), tail, grouped=True)
            left(tok.at[0, 0:8], u_s.at[0], head)
            left(tok.at[0, 0:7], u_s.at[1], tail)
        send(us.at[step], zf.at[step], v_s.at[step], v_r.at[step], q - 1, s, head)

    def arrive(step):
        arrived(zf.at[step], v_r.at[step], q < nq - 1)

        @pl.when(q == nq - 1)
        def _():
            zf[step] = fresh[step]

    embed(0, 0, 1, 2, 3)
    onward(0, 0)
    cross_out(1)
    embed(0, 4, 5, 6, 7)
    onward(1, 0)
    project(0)
    cross_in(0)
    cross_out(2)
    pass_on(0, 0)
    project(1, 2)
    onward(2, 0)
    attend(0, 1)
    pass_on(1, 0)
    onward(3, 0)
    pass_on(0, 2)
    far_in(0, 0)
    cross_in(1)
    cross_out(3)
    pass_on(2, 0)
    far_in(1, 0)
    pass_on(3, 0)
    attend(0, 0)
    onward(0, 1)
    pass_on(0, 1)
    pass_on(1, 2)
    far_in(2, 0)
    cross_in(2)
    pass_on(1, 1)
    far_in(3, 0)
    pass_on(0, 3)
    onward(1, 1)
    pass_on(2, 1)
    pass_on(2, 2)
    far_in(0, 1)
    cross_in(3)
    pass_on(3, 1)
    onward(2, 1)
    pass_on(1, 3)
    far_in(1, 1)
    pass_on(0, 4)
    complete(0)
    middle(0)
    onward(3, 1)
    pass_on(2, 3)
    pass_on(3, 2)
    far_in(2, 1)
    far_in(3, 1)
    pass_on(1, 4)
    complete(1)
    queries(0)
    relay(0, 1, 2)
    pass_on(3, 3)
    pass_on(2, 4)
    relay(0, 0, 3)
    pass_on(3, 4)
    complete(2)
    relayed(0, 1, 2, 0, 3)
    keys(0, (0, 10))
    values(0, (0, 10))
    blend()
    complete(3)
    final(0)
    embed(1, 0, 1, 2, 3)
    embed(1, 4, 5, 6, 7)
    project(0, 1, 2)
    attend(1, 1)
    attend(1, 0)
    arrive(0)
    zcur[...] = zf[0]
    middle(1)
    queries(1)
    keys(1, (4, 6))
    values(1, (4, 6))
    relay(1, 1, 2)
    relayed(1, 1, 2)
    keys(1, (2, 4), (6, 8))
    values(1, (2, 4), (6, 8))
    relay(1, 0, 3)
    relayed(1, 0, 3)
    keys(1, (0, 2), (8, 10))
    values(1, (0, 2), (8, 10))
    blend()
    final(1)
    arrive(1)
    after[...] = zf[1]

    for copy, when in sends:
        if when is None:
            copy.wait_send()
        else:
            pl.when(when)(copy.wait_send)


def hand_out(after_in, velocity_in, after, velocity):
    after[...] = after_in[...]
    velocity[...] = velocity_in[...]


def solution(mesh):
    nq = mesh.shape["queue"]

    def local(latents, fresh_noise, levels, modulation_weight, embed_weight, attention_weights, final_weight):
        dma = pltpu.SemaphoreType.DMA
        vmem = pl.BlockSpec(memory_space=pltpu.VMEM)
        after, velocity = pl.pallas_call(
            functools.partial(kernel, nq),
            out_shape=(
                jax.ShapeDtypeStruct((16, ROWS), F32),
                jax.ShapeDtypeStruct((STEPS, 16, ROWS), F32),
            ),
            in_specs=[pl.BlockSpec(memory_space=pltpu.SMEM)] + [vmem] * 5 + [pl.BlockSpec(memory_space=pl.ANY)],
            out_specs=(vmem, vmem),
            scratch_shapes=[
                pltpu.VMEM((16, SPACE, ROWS, D), BF16),
                pltpu.VMEM((3, 3, ROWS, D), BF16),
                pltpu.VMEM((STEPS, SPACE, 16, ROWS), BF16),
                pltpu.VMEM((STEPS, 16, ROWS), F32),
                pltpu.VMEM((16, ROWS), F32),
                pltpu.VMEM((SPACE, 1, 2 * D), F32),
                pltpu.VMEM((8, 2 * D), F32),
                pltpu.VMEM((1, 2 * D), F32),
                pltpu.VMEM((6, 1, D), F32),
                pltpu.VMEM((SPACE, ROWS, D), BF16),
                pltpu.VMEM((SPACE * ROWS, 144), BF16),
                pltpu.VMEM((SPACE * ROWS, 144), BF16),
                pltpu.VMEM((SPACE * ROWS, 144), BF16),
                pltpu.VMEM((STEPS, SPACE, 4, 16, 128), BF16),
                pltpu.VMEM((STEPS, SPACE, 4, 16, 128), BF16),
                pltpu.VMEM((ROWS, D), F32),
                pltpu.VMEM((STEPS, 10, ROWS, D), BF16),
                pltpu.VMEM((3, ROWS, THIRD), BF16),
                pltpu.VMEM((3, ROWS, THIRD), BF16),
                pltpu.VMEM((SLOTS, ROWS, 128), F32),
                pltpu.VMEM((3, SLOTS, ROWS, THIRD), BF16),
                pltpu.VMEM((3, THIRD, 128), BF16),
                pltpu.VMEM((3, 128, THIRD), BF16),
                pltpu.VMEM((2, 16, ROWS), BF16),
                pltpu.VMEM((STEPS, 16, ROWS), F32),
                dma((6,)),
                dma((1,)), dma((1,)),
                dma((1,)), dma((1,)),
                dma((2,)), dma((ROUNDS,)), dma((ROUNDS, 2, 2)), dma((ROUNDS, 2)),
                dma((ROUNDS, 5)), dma((ROUNDS, 2)),
                dma((STEPS,)), dma((STEPS, 2)),
                dma((STEPS, 4)), dma((STEPS, 4)),
                dma((STEPS, 5)), dma((STEPS, 5)),
                dma((2,)), dma((3,)),
                dma((STEPS,)), dma((STEPS,)),
            ],
            compiler_params=pltpu.CompilerParams(
                collective_id=0, has_side_effects=True, vmem_limit_bytes=56 << 20
            ),
            name="denoise",
        )(
            levels, latents[0].T, jnp.swapaxes(fresh_noise, 1, 2), modulation_weight.T, embed_weight,
            final_weight.T, attention_weights.reshape(8, 3, ROWS, D),
        )
        after, velocity = pl.pallas_call(
            hand_out, out_shape=(after, velocity), in_specs=[vmem] * 2, out_specs=(vmem, vmem), name="hand_out"
        )(after, velocity)
        return after.T[None], jnp.swapaxes(velocity, 1, 2)[:, None]

    in_specs = (
        P("queue", "space", None),
        P(None, "space", None),
        P(),
        P(None, "space"),
        P(),
        P(None, "space", None),
        P(),
    )
    out_specs = (P("queue", "space", None), P(None, "queue", "space", None))
    return jax.shard_map(local, mesh=mesh, in_specs=in_specs, out_specs=out_specs, check_vma=False)
```
